128 devices in a mesh: group: 4 (over z_lo, core), dp: 32 (over z_hi, y, x).
Axes of the slice: x: 4, y: 4, z: 4 (z_hi: 2, z_lo: 2; z = z_hi * 2 + z_lo), core: 2. Of those that a mesh axis runs over, the one named last changes fastest.
Arguments:
- teacher_feat: bfloat16 [256, 257, 4096], P(('dp', 'group')), may hold values from -6 to 6
- teacher_bottleneck: bfloat16 [4096, 256], replicated, may hold values from -0.09375 to 0.09375
- teacher_proto: bfloat16 [256, 65536], P(None, 'dp')
- student_feat: bfloat16 [4, 256, 257, 1024], P('group', 'dp'), may hold values from -6 to 6
- student_bottleneck: bfloat16 [4, 1024, 256], P('group'), may hold values from -0.1875 to 0.1875
- student_proto: bfloat16 [4, 256, 65536], P('group', None, 'dp')
- mask_index: int32 [256, 16], P('dp'), may hold values from 1 to 256, as said below
- mask_count: int32 [256], replicated, may hold values from 1 to 16, as said below
Outputs:
- grad_proto: float32 [4, 256, 65536], P('group', None, 'dp')
- grad_bottleneck: float32 [4, 1024, 256], P('group', 'dp')
- grad_rows: bfloat16 [4, 256, 17, 1024], P('group', 'dp')
The draws below stay inside these ranges and needn't reach their ends.
Inputs may be any that keep to these rules, and one draw needn't show every extreme that they name: `mask_index`: the mask slots of one image name distinct patches. `mask_count`: some image has all 16 slots live.
All inputs are finite; a program needn't handle non-finite values.
Results may differ from the reference program's by a relative error of at most 0.039.
Values may be sent and summed in bfloat16 or wider, within the bound.
No kernel may reach another device: no remote copies, remote signals or barrier semaphores. Data moves between devices by JAX's collectives and lax.ppermute only.
A program may use at most 128 MiB of HBM per device.

```python
import jax
import jax.numpy as jnp
from jax import lax

DT = 4096
DS = 1024
K = 256
PROTO = 65536
PATCHES = 256
MASKED = 16
IMAGES = 256
N_GROUP = 4


def draw_teacher_proto(key, part):
    key = jax.random.fold_in(key, 11)
    values = 0.3 * jax.random.normal(key, (K, PROTO), jnp.float32)
    return values.astype(jnp.bfloat16)


def draw_student_proto(key, part):
    key = jax.random.fold_in(key, 12)
    values = 0.3 * jax.random.normal(key, (N_GROUP, K, PROTO), jnp.float32)
    return values.astype(jnp.bfloat16)


def draw_mask_index(key, part):
    key = jax.random.fold_in(key, 13)
    image_keys = jax.random.split(key, IMAGES)
    return jax.vmap(lambda single: jax.random.permutation(single, PATCHES)[:MASKED] + 1)(image_keys).astype(jnp.int32)


def draw_mask_count(key, part):
    key = jax.random.fold_in(key, 14)
    counts = jax.random.randint(key, (IMAGES,), 1, MASKED + 1)
    chosen = jax.random.randint(jax.random.fold_in(key, 1), (), 0, IMAGES)
    return jnp.where(jnp.arange(IMAGES) == chosen, MASKED, counts).astype(jnp.int32)


def steps_of(key, shape, shards, least, top_value):
    level, own = 1.0, jax.random.fold_in(key, 6)
    for dim, blocks in shards:
        draws = jnp.exp(jax.random.uniform(jax.random.fold_in(own, dim), (blocks,), jnp.float32, least / len(shards), top_value / len(shards)))
        level = level * jnp.repeat(draws, shape[dim] // blocks).reshape([-1 if axis == dim else 1 for axis in range(len(shape))])
    return level


def gaussian(stream_key, dims, deviation, reach, cuts=(), kind=jnp.bfloat16):
    factor_of = steps_of(stream_key, dims, cuts, -0.22, 0.18) if cuts else 1.0
    array = jax.random.normal(stream_key, dims, jnp.float32) * deviation * factor_of
    return jnp.minimum(jnp.maximum(array, -reach), reach).astype(kind)


def setup_inputs(seed: int = 0) -> dict:
    key_of = jax.random.split(jax.random.key(seed), 9)
    teacher_feat = gaussian(key_of[0], (IMAGES, PATCHES + 1, DT), 1.0, 6.0, ((0, 128),))
    teacher_bottleneck = gaussian(key_of[1], (DT, K), DT ** -0.5, 0.09375)
    teacher_proto = draw_teacher_proto(jax.random.fold_in(key_of[8], 71), 0)
    student_feat = gaussian(key_of[3], (N_GROUP, IMAGES, PATCHES + 1, DS), 1.0, 6.0, ((0, 4), (1, 32)))
    student_bottleneck = gaussian(key_of[4], (N_GROUP, DS, K), DS ** -0.5, 0.1875, ((0, 4),))
    student_proto = draw_student_proto(jax.random.fold_in(key_of[8], 71), 0)
    mask_index = draw_mask_index(jax.random.fold_in(key_of[8], 71), 0)
    mask_count = draw_mask_count(jax.random.fold_in(key_of[8], 71), 0)
    return {"teacher_feat": teacher_feat, "teacher_bottleneck": teacher_bottleneck, "teacher_proto": teacher_proto, "student_feat": student_feat, "student_bottleneck": student_bottleneck, "student_proto": student_proto, "mask_index": mask_index, "mask_count": mask_count}


teacher_temp = 0.05
student_temp = 0.1
norm_eps = 1e-06

def pick_rows(features, mask_index):
    picked = jax.vmap(lambda image_rows, chosen: jnp.take(image_rows, chosen, axis=0))(features, mask_index)
    return jnp.concatenate([features[:, :1, :], picked], axis=1)

def row_weights(mask_count, slot_count):
    counts = mask_count.astype(jnp.float32)[:, None]
    position = jnp.arange(slot_count)[None, :]
    inside = jnp.where(position.astype(jnp.float32) <= counts, 1.0 / counts, 0.0)
    return jnp.where(position == 0, 1.0, inside).astype(jnp.float32)

def normalize_rows(projected):
    lengths = jnp.sqrt(lax.optimization_barrier(jnp.sum(projected * projected, axis=-1, keepdims=True)) + norm_eps)
    return (projected / lengths, lengths)

def reference(teacher_feat, teacher_bottleneck, teacher_proto, student_feat, student_bottleneck, student_proto, mask_index, mask_count):
    slot_count = mask_index.shape[1] + 1
    teacher_rows = pick_rows(teacher_feat, mask_index).reshape(-1, teacher_feat.shape[-1])
    teacher_unit = normalize_rows(jnp.dot(teacher_rows, teacher_bottleneck, preferred_element_type=jnp.float32))[0].astype(jnp.bfloat16)
    weights = row_weights(mask_count, slot_count).reshape(-1)
    groups = student_feat.shape[0]
    student_rows = jax.vmap(pick_rows, in_axes=(0, None))(student_feat, mask_index).reshape(groups, -1, student_feat.shape[-1])
    projected = jnp.einsum('grd,gdk->grk', student_rows.astype(jnp.float32), student_bottleneck.astype(jnp.float32))
    student_float, lengths = normalize_rows(projected)
    student_unit = student_float.astype(jnp.bfloat16)
    rows_total = teacher_unit.shape[0]
    bottleneck_width = teacher_unit.shape[1]
    block_rows = 32 * slot_count
    blocks = rows_total // block_rows
    teacher_blocks = teacher_unit.reshape(blocks, block_rows, bottleneck_width)
    student_blocks = student_unit.reshape(groups, blocks, block_rows, bottleneck_width).transpose(1, 0, 2, 3)
    weight_blocks = weights.reshape(blocks, block_rows)

    def step_block(grad_carry, inputs):
        teacher_block, student_block, weight_block = inputs
        teacher_probs = jax.nn.softmax(jnp.dot(teacher_block, teacher_proto, preferred_element_type=jnp.float32) / teacher_temp, axis=-1)
        updates = []
        row_terms = []
        for member in range(groups):
            student_probs = jax.nn.softmax(jnp.dot(student_block[member], student_proto[member], preferred_element_type=jnp.float32) / student_temp, axis=-1)
            logit_grad = (weight_block[:, None] * (student_probs - teacher_probs) / student_temp).astype(jnp.bfloat16)
            updates.append(lax.dot_general(student_block[member], logit_grad, (((0,), (0,)), ((), ())), preferred_element_type=jnp.float32))
            row_terms.append(lax.dot_general(logit_grad, student_proto[member], (((1,), (1,)), ((), ())), preferred_element_type=jnp.float32))
        return (grad_carry + jnp.stack(updates), jnp.stack(row_terms))
    start_grad = jnp.zeros((groups, bottleneck_width, teacher_proto.shape[1]), jnp.float32)
    grad_proto, all_terms = lax.scan(step_block, start_grad, (teacher_blocks, student_blocks, weight_blocks))
    feature_grad = all_terms.transpose(1, 0, 2, 3).reshape(groups, rows_total, bottleneck_width)
    along_unit = lax.optimization_barrier(jnp.sum(student_float * feature_grad, axis=-1, keepdims=True))
    unit_grad = ((feature_grad - student_float * along_unit) / lengths).astype(jnp.bfloat16)
    grad_bottleneck = jnp.einsum('grd,grk->gdk', student_rows.astype(jnp.float32), unit_grad.astype(jnp.float32))
    grad_rows = jnp.einsum('grk,gdk->grd', unit_grad.astype(jnp.float32), student_bottleneck.astype(jnp.float32)).astype(jnp.bfloat16)
    grad_rows = grad_rows.reshape(groups, -1, slot_count, student_feat.shape[-1])
    return (grad_proto, grad_bottleneck, grad_rows)
```

```python
import functools

import jax
import jax.numpy as jnp
from jax import lax
from jax.experimental import pallas as pl
from jax.experimental.pallas import tpu as pltpu
from jax.sharding import PartitionSpec as P

teacher_temp = 0.05
student_temp = 0.1
norm_eps = 1e-06
log2e = 1.4426950408889634
never = 1e30
bf16 = jnp.bfloat16
f32 = jnp.float32


def normalize_rows(projected):
    lengths = jnp.sqrt(jnp.sum(projected * projected, axis=-1, keepdims=True) + norm_eps)
    return (projected / lengths, lengths)


def column_of(row):
    wide = jnp.broadcast_to(row, (128, row.shape[1]))
    return jnp.transpose(wide)[:, :1]


def row_of(column):
    wide = jnp.broadcast_to(column, (column.shape[0], 128))
    return jnp.transpose(wide)[:1, :]


def stats_kernel(scale, rows_ref, proto_ref, lse_ref):
    logits = jnp.dot(rows_ref[...], proto_ref[...], preferred_element_type=f32)
    peak = jnp.max(logits, axis=-1, keepdims=True)
    total = jnp.sum(jnp.exp2((logits - peak) * scale), axis=-1, keepdims=True)
    lse_ref[0] = row_of(peak * scale + jnp.log2(total))


def local_lse(rows, proto, temp, block):
    count, width = rows.shape
    steps = count // block
    out = pl.pallas_call(
        functools.partial(stats_kernel, log2e / temp),
        grid=(steps,),
        in_specs=[
            pl.BlockSpec((block, width), lambda i: (i, 0)),
            pl.BlockSpec(proto.shape, lambda i: (0, 0)),
        ],
        out_specs=pl.BlockSpec((1, 1, block), lambda i: (i, 0, 0)),
        out_shape=jax.ShapeDtypeStruct((steps, 1, block), f32),
        compiler_params=pltpu.CompilerParams(vmem_limit_bytes=48 * 2**20),
        cost_estimate=pl.CostEstimate(
            flops=2 * count * proto.size, bytes_accessed=2 * (rows.size + proto.size), transcendentals=count * proto.shape[1]
        ),
    )(rows, proto)
    return out.reshape(1, count)


def grads_kernel(tile, teacher_ref, student_ref, shift_t_ref, shift_s_ref, proto_t_ref, proto_s_ref, proto_sT_ref,
                 grad_ref, rows_ref):
    @pl.when(pl.program_id(0) == 0)
    def _():
        grad_ref[...] = jnp.zeros_like(grad_ref)

    teacher, student = teacher_ref[...], student_ref[...]
    student_T = jnp.transpose(student)
    shift_t, shift_s = column_of(shift_t_ref[0]), column_of(shift_s_ref[0])
    total = jnp.zeros(rows_ref.shape, f32)
    for start in range(0, proto_t_ref.shape[1], tile):
        cols = slice(start, start + tile)
        logits_t = jnp.dot(teacher, proto_t_ref[:, cols], preferred_element_type=f32)
        logits_s = jnp.dot(student, proto_s_ref[:, cols], preferred_element_type=f32)
        grad = (
            jnp.exp2(logits_s * (log2e / student_temp) - shift_s)
            - jnp.exp2(logits_t * (log2e / teacher_temp) - shift_t)
        ).astype(bf16)
        grad_ref[:, cols] += jnp.dot(student_T, grad, preferred_element_type=f32)
        total += jnp.dot(grad, proto_sT_ref[cols, :], preferred_element_type=f32)
    rows_ref[...] = total.astype(bf16)


def gradients(teacher, student, shift_t, shift_s, proto_t, proto_s, proto_sT, block, tile=256):
    count, width = student.shape
    steps = count // block
    columns = proto_s.shape[1]
    rows_spec = pl.BlockSpec((block, width), lambda i: (i, 0))
    shift_spec = pl.BlockSpec((1, 1, block), lambda i: (i, 0, 0))
    whole = lambda array: pl.BlockSpec(array.shape, lambda i: (0, 0))
    return pl.pallas_call(
        functools.partial(grads_kernel, tile),
        grid=(steps,),
        in_specs=[rows_spec, rows_spec, shift_spec, shift_spec, whole(proto_t), whole(proto_s), whole(proto_sT)],
        out_specs=[pl.BlockSpec((width, columns), lambda i: (0, 0)), rows_spec],
        out_shape=[jax.ShapeDtypeStruct((width, columns), f32), jax.ShapeDtypeStruct((count, width), bf16)],
        compiler_params=pltpu.CompilerParams(vmem_limit_bytes=48 * 2**20),
        cost_estimate=pl.CostEstimate(
            flops=8 * count * proto_s.size, bytes_accessed=8 * proto_s.size, transcendentals=2 * count * columns
        ),
    )(teacher, student, shift_t.reshape(steps, 1, block), shift_s.reshape(steps, 1, block), proto_t, proto_s, proto_sT)


def to_all(block, parts):
    return lax.all_to_all(jnp.broadcast_to(block[None], (parts,) + block.shape), "dp", 0, 0)


def slots_of(counts, capacity):
    lengths = counts + 1
    ends = jnp.cumsum(lengths, axis=-1)
    starts = ends - lengths
    slot = jnp.arange(capacity)[None, :, None]
    inside = (slot >= starts[:, None, :]) & (slot < ends[:, None, :])
    place = jnp.sum(jnp.where(inside, slot - starts[:, None, :], 0), axis=-1)
    return inside, place


def on_device(
    teacher_feat,
    teacher_bottleneck,
    teacher_proto,
    student_feat,
    student_bottleneck,
    student_proto,
    mask_index,
    mask_count,
    *,
    parts,
    capacity,
):
    images, masked = mask_index.shape
    slot_count = masked + 1
    width = student_bottleneck.shape[-1]
    student_feat, student_bottleneck, student_proto = student_feat[0], student_bottleneck[0], student_proto[0]
    teacher_images = teacher_feat.shape[0]
    me = lax.axis_index("dp")
    capacity = capacity or images * slot_count
    block = 256

    counts = mask_count.reshape(parts, images)
    inside, place = slots_of(counts, capacity)
    live = jnp.any(inside, axis=-1)
    share = jnp.sum(jnp.where(inside, 1.0 / counts.astype(f32)[:, None, :], 0.0), axis=-1)
    weight = jnp.where(place == 0, 1.0, share)
    log_weight = jnp.where(live, jnp.log2(jnp.where(live, weight, 1.0) / student_temp), -never).reshape(-1)
    my_inside = lax.dynamic_index_in_dim(inside, me, 0, keepdims=False)
    my_place = lax.dynamic_index_in_dim(place, me, 0, keepdims=False)
    my_image = jnp.sum(jnp.where(my_inside, jnp.arange(images), 0), axis=-1)
    indices = jnp.concatenate([jnp.zeros((images, 1), jnp.int32), mask_index], axis=1)
    picks = jnp.where(
        jnp.any(my_inside, axis=-1)[:, None],
        (my_image * slot_count + my_place)[:, None] == jnp.arange(images * slot_count)[None, :],
        False,
    )
    my_rows = jnp.sum(jnp.where(picks, indices.reshape(1, -1), 0), axis=-1)

    first_image = lax.axis_index("group") * teacher_images
    teacher_index = lax.dynamic_slice_in_dim(indices, first_image, teacher_images, 0)
    teacher_rows = teacher_feat[jnp.arange(teacher_images)[:, None], teacher_index].reshape(-1, teacher_feat.shape[-1])
    teacher_unit = normalize_rows(jnp.dot(teacher_rows, teacher_bottleneck, preferred_element_type=f32))[0].astype(bf16)
    group_teacher = lax.all_gather(teacher_unit, "group", axis=0, tiled=True)
    group_teacher = jnp.dot(picks.astype(bf16), group_teacher, preferred_element_type=f32).astype(bf16)

    student_rows = student_feat[my_image, my_rows]
    student_float, lengths = normalize_rows(jnp.dot(student_rows, student_bottleneck, preferred_element_type=f32))
    student_unit = student_float.astype(bf16)

    every_teacher = to_all(group_teacher, parts).reshape(-1, width)
    every_student = to_all(student_unit, parts).reshape(-1, width)

    lse_t = local_lse(every_teacher, teacher_proto, teacher_temp, block)
    lse_s = local_lse(every_student, student_proto, student_temp, block)
    every_lse = to_all(jnp.concatenate([lse_t, lse_s], axis=1), parts)
    top = jnp.max(every_lse, axis=0)
    lse = top + jnp.log2(jnp.sum(jnp.exp2(every_lse - top), axis=0))
    rows_total = every_student.shape[0]
    shift_t = lse[0, :rows_total] - log_weight
    shift_s = lse[0, rows_total:] - log_weight

    grad_proto, row_terms = gradients(
        every_teacher, every_student, shift_t, shift_s, teacher_proto, student_proto, student_proto.T, block
    )
    terms = lax.all_to_all(row_terms.reshape(parts, capacity, width), "dp", 0, 0)
    feature_grad = jnp.sum(terms.astype(f32), axis=0)
    along_unit = jnp.sum(student_float * feature_grad, axis=-1, keepdims=True)
    unit_grad = ((feature_grad - student_float * along_unit) / lengths).astype(bf16)
    partial_bottleneck = lax.dot_general(
        student_rows, unit_grad, (((0,), (0,)), ((), ())), preferred_element_type=f32
    ).astype(bf16)
    pieces = lax.all_to_all(partial_bottleneck.reshape(parts, -1, width), "dp", 0, 0)
    grad_bottleneck = jnp.sum(pieces.astype(f32), axis=0)
    spread_grad = lax.dot_general(
        picks.astype(bf16), unit_grad, (((0,), (0,)), ((), ())), preferred_element_type=f32
    ).astype(bf16)
    grad_rows = lax.dot_general(
        spread_grad, student_bottleneck, (((1,), (1,)), ((), ())), preferred_element_type=f32
    ).astype(bf16)
    return (
        grad_proto[None],
        grad_bottleneck[None],
        grad_rows.reshape(1, images, slot_count, grad_rows.shape[-1]),
    )


def solution(mesh):
    in_specs = (
        P(("dp", "group"), None, None),
        P(),
        P(None, "dp"),
        P("group", "dp", None, None),
        P("group", None, None),
        P("group", None, "dp"),
        P("dp", None),
        P(),
    )
    out_specs = (P("group", None, "dp"), P("group", "dp", None), P("group", "dp", None, None))
    step = functools.partial(on_device, parts=mesh.shape["dp"], capacity=None)
    return jax.shard_map(step, mesh=mesh, in_specs=in_specs, out_specs=out_specs, check_vma=False)
```

```python
import functools

import jax
import jax.numpy as jnp
from jax import lax
from jax.experimental import pallas as pl
from jax.experimental.pallas import tpu as pltpu
from jax.sharding import PartitionSpec as P

teacher_temp = 0.05
student_temp = 0.1
norm_eps = 1e-06
log2e = 1.4426950408889634
never = 1e30
bf16 = jnp.bfloat16
f32 = jnp.float32


def normalize_rows(projected):
    lengths = jnp.sqrt(jnp.sum(projected * projected, axis=-1, keepdims=True) + norm_eps)
    return (projected / lengths, lengths)


def column_of(row):
    wide = jnp.broadcast_to(row, (128, row.shape[1]))
    return jnp.transpose(wide)[:, :1]


def row_of(column):
    wide = jnp.broadcast_to(column, (column.shape[0], 128))
    return jnp.transpose(wide)[:1, :]


def stats_kernel(scale, rows_ref, proto_ref, lse_ref):
    logits = jnp.dot(rows_ref[...], proto_ref[...], preferred_element_type=f32)
    peak = jnp.max(logits, axis=-1, keepdims=True)
    total = jnp.sum(jnp.exp2((logits - peak) * scale), axis=-1, keepdims=True)
    lse_ref[0] = row_of(peak * scale + jnp.log2(total))


def local_lse(rows, proto, temp, block):
    count, width = rows.shape
    steps = count // block
    out = pl.pallas_call(
        functools.partial(stats_kernel, log2e / temp),
        grid=(steps,),
        in_specs=[
            pl.BlockSpec((block, width), lambda i: (i, 0)),
            pl.BlockSpec(proto.shape, lambda i: (0, 0)),
        ],
        out_specs=pl.BlockSpec((1, 1, block), lambda i: (i, 0, 0)),
        out_shape=jax.ShapeDtypeStruct((steps, 1, block), f32),
        compiler_params=pltpu.CompilerParams(vmem_limit_bytes=48 * 2**20),
        cost_estimate=pl.CostEstimate(
            flops=2 * count * proto.size, bytes_accessed=2 * (rows.size + proto.size), transcendentals=count * proto.shape[1]
        ),
    )(rows, proto)
    return out.reshape(1, count)


def grads_kernel(tile, teacher_ref, student_ref, shift_t_ref, shift_s_ref, proto_t_ref, proto_s_ref, proto_sT_ref,
                 grad_ref, rows_ref):
    @pl.when(pl.program_id(0) == 0)
    def _():
        grad_ref[...] = jnp.zeros_like(grad_ref)

    teacher, student = teacher_ref[...], student_ref[...]
    student_T = jnp.transpose(student)
    shift_t, shift_s = column_of(shift_t_ref[0]), column_of(shift_s_ref[0])
    total = jnp.zeros(rows_ref.shape, f32)
    for start in range(0, proto_t_ref.shape[1], tile):
        cols = slice(start, start + tile)
        logits_t = jnp.dot(teacher, proto_t_ref[:, cols], preferred_element_type=f32)
        logits_s = jnp.dot(student, proto_s_ref[:, cols], preferred_element_type=f32)
        grad = (
            jnp.exp2(logits_s * (log2e / student_temp) - shift_s)
            - jnp.exp2(logits_t * (log2e / teacher_temp) - shift_t)
        ).astype(bf16)
        grad_ref[:, cols] += jnp.dot(student_T, grad, preferred_element_type=f32)
        total += jnp.dot(grad, proto_sT_ref[cols, :], preferred_element_type=f32)
    rows_ref[...] = total.astype(bf16)


def gradients(teacher, student, shift_t, shift_s, proto_t, proto_s, proto_sT, block, tile=256):
    count, width = student.shape
    steps = count // block
    columns = proto_s.shape[1]
    rows_spec = pl.BlockSpec((block, width), lambda i: (i, 0))
    shift_spec = pl.BlockSpec((1, 1, block), lambda i: (i, 0, 0))
    whole = lambda array: pl.BlockSpec(array.shape, lambda i: (0, 0))
    return pl.pallas_call(
        functools.partial(grads_kernel, tile),
        grid=(steps,),
        in_specs=[rows_spec, rows_spec, shift_spec, shift_spec, whole(proto_t), whole(proto_s), whole(proto_sT)],
        out_specs=[pl.BlockSpec((width, columns), lambda i: (0, 0)), rows_spec],
        out_shape=[jax.ShapeDtypeStruct((width, columns), f32), jax.ShapeDtypeStruct((count, width), bf16)],
        compiler_params=pltpu.CompilerParams(vmem_limit_bytes=48 * 2**20),
        cost_estimate=pl.CostEstimate(
            flops=8 * count * proto_s.size, bytes_accessed=8 * proto_s.size, transcendentals=2 * count * columns
        ),
    )(teacher, student, shift_t.reshape(steps, 1, block), shift_s.reshape(steps, 1, block), proto_t, proto_s, proto_sT)


def to_all(block, parts):
    return lax.all_to_all(jnp.broadcast_to(block[None], (parts,) + block.shape), "dp", 0, 0)


def slots_of(counts, capacity):
    lengths = counts + 1
    ends = jnp.cumsum(lengths, axis=-1)
    starts = ends - lengths
    slot = jnp.arange(capacity)[None, :, None]
    inside = (slot >= starts[:, None, :]) & (slot < ends[:, None, :])
    live = jnp.any(inside, axis=-1)
    image = jnp.sum(jnp.where(inside, jnp.arange(counts.shape[1]), 0), axis=-1)
    place = jnp.sum(jnp.where(inside, slot - starts[:, None, :], 0), axis=-1)
    share = jnp.sum(jnp.where(inside, 1.0 / counts.astype(f32)[:, None, :], 0.0), axis=-1)
    return image, place, jnp.where(place == 0, 1.0, share), live


def packed_step(
    teacher_feat,
    teacher_bottleneck,
    teacher_proto,
    student_feat,
    student_bottleneck,
    student_proto,
    mask_index,
    mask_count,
    *,
    parts,
    group,
    capacity,
):
    images, masked = mask_index.shape
    slot_count = masked + 1
    width = student_bottleneck.shape[-1]
    teacher_images = teacher_feat.shape[0]
    teacher_count = teacher_images * slot_count
    padded_count = -(-teacher_count // 8) * 8
    me = lax.axis_index("dp")

    indices = jnp.concatenate([jnp.zeros((images, 1), jnp.int32), mask_index], axis=1)
    first_image = lax.axis_index("group") * teacher_images
    teacher_index = lax.dynamic_slice_in_dim(indices, first_image, teacher_images, 0)
    teacher_rows = teacher_feat[jnp.arange(teacher_images)[:, None], teacher_index].reshape(-1, teacher_feat.shape[-1])
    teacher_unit = normalize_rows(jnp.dot(teacher_rows, teacher_bottleneck, preferred_element_type=f32))[0].astype(bf16)
    teacher_unit = jnp.pad(teacher_unit, ((0, padded_count - teacher_count), (0, 0)))
    member_teacher = to_all(teacher_unit, parts).reshape(-1, width)

    image, place, weight, live = slots_of(mask_count.reshape(parts, images), capacity)
    log_weight = jnp.where(live, jnp.log2(weight / student_temp), -never).reshape(-1)
    mine = lambda array: lax.dynamic_index_in_dim(array, me, 0, keepdims=False)
    my_image, my_place, my_live = mine(image), mine(place), mine(live)
    spread = ((my_image * slot_count + my_place)[:, None] == jnp.arange(images * slot_count)) & my_live[:, None]
    my_rows = jnp.sum(jnp.where(spread, indices.reshape(1, -1), 0), axis=-1)
    source = (image // teacher_images) * padded_count + (image % teacher_images) * slot_count + place
    picks = (source[:, :, None] == jnp.arange(group * padded_count)) & live[:, :, None]

    student_rows = student_feat[my_image, my_rows]
    student_float, lengths = normalize_rows(jnp.dot(student_rows, student_bottleneck, preferred_element_type=f32))
    student_unit = student_float.astype(bf16)
    every_student = to_all(student_unit, parts).reshape(-1, width)

    group_teacher = lax.all_gather(member_teacher, "group", axis=0).reshape(group, parts, padded_count, width)
    group_teacher = group_teacher.transpose(1, 0, 2, 3).reshape(parts, group * padded_count, width)
    every_teacher = lax.dot_general(
        picks.astype(bf16), group_teacher, (((2,), (1,)), ((0,), (0,))), preferred_element_type=f32
    ).astype(bf16).reshape(-1, width)

    member_lse = local_lse(member_teacher, teacher_proto, teacher_temp, 256)
    group_lse = lax.all_gather(member_lse[0], "group", axis=0).reshape(group, parts, padded_count)
    group_lse = group_lse.transpose(1, 0, 2).reshape(parts, 1, group * padded_count)
    lse_t = jnp.sum(jnp.where(picks, group_lse, 0.0), axis=-1).reshape(1, -1)
    lse_s = local_lse(every_student, student_proto, student_temp, 256)
    every_lse = to_all(jnp.concatenate([lse_t, lse_s], axis=1), parts)
    top = jnp.max(every_lse, axis=0)
    lse = top + jnp.log2(jnp.sum(jnp.exp2(every_lse - top), axis=0))
    rows_total = every_student.shape[0]
    shift_t = lse[0, :rows_total] - log_weight
    shift_s = lse[0, rows_total:] - log_weight

    grad_proto, row_terms = gradients(
        every_teacher, every_student, shift_t, shift_s, teacher_proto, student_proto, student_proto.T, 256
    )
    terms = lax.all_to_all(row_terms.reshape(parts, capacity, width), "dp", 0, 0)
    feature_grad = jnp.sum(terms.astype(f32), axis=0)
    along_unit = jnp.sum(student_float * feature_grad, axis=-1, keepdims=True)
    unit_grad = ((feature_grad - student_float * along_unit) / lengths).astype(bf16)
    partial_bottleneck = lax.dot_general(
        student_rows, unit_grad, (((0,), (0,)), ((), ())), preferred_element_type=f32
    ).astype(bf16)
    pieces = lax.all_to_all(partial_bottleneck.reshape(parts, -1, width), "dp", 0, 0)
    grad_bottleneck = jnp.sum(pieces.astype(f32), axis=0)
    spread_grad = lax.dot_general(
        spread.astype(bf16), unit_grad, (((0,), (0,)), ((), ())), preferred_element_type=f32
    ).astype(bf16)
    grad_rows = lax.dot_general(
        spread_grad, student_bottleneck, (((1,), (1,)), ((), ())), preferred_element_type=f32
    ).astype(bf16)
    return grad_proto, grad_bottleneck, grad_rows.reshape(images, slot_count, grad_rows.shape[-1])


def on_device(
    teacher_feat,
    teacher_bottleneck,
    teacher_proto,
    student_feat,
    student_bottleneck,
    student_proto,
    mask_index,
    mask_count,
    *,
    parts,
    group,
):
    images, masked = mask_index.shape
    full = images * (masked + 1)
    capacities = [c for c in (96, 104, 112, 120) if c < full] + [full]
    needed = jnp.max(jnp.sum(mask_count.reshape(parts, images) + 1, axis=-1))
    branch = jnp.sum((needed > jnp.array(capacities[:-1])).astype(jnp.int32))
    outs = lax.switch(
        branch,
        [functools.partial(packed_step, parts=parts, group=group, capacity=c) for c in capacities],
        teacher_feat,
        teacher_bottleneck,
        teacher_proto,
        student_feat[0],
        student_bottleneck[0],
        student_proto[0],
        mask_index,
        mask_count,
    )
    return tuple(out[None] for out in outs)


def solution(mesh):
    in_specs = (
        P(("dp", "group"), None, None),
        P(),
        P(None, "dp"),
        P("group", "dp", None, None),
        P("group", None, None),
        P("group", None, "dp"),
        P("dp", None),
        P(),
    )
    out_specs = (P("group", None, "dp"), P("group", "dp", None), P("group", "dp", None, None))
    step = functools.partial(on_device, parts=mesh.shape["dp"], group=mesh.shape["group"])
    return jax.shard_map(step, mesh=mesh, in_specs=in_specs, out_specs=out_specs, check_vma=False)
```

```python
import functools

import jax
import jax.numpy as jnp
from jax import lax
from jax.experimental import pallas as pl
from jax.experimental.pallas import tpu as pltpu
from jax.sharding import PartitionSpec as P

teacher_temp = 0.05
student_temp = 0.1
norm_eps = 1e-06
log2e = 1.4426950408889634
never = 1e30
bf16 = jnp.bfloat16
f32 = jnp.float32


def normalize_rows(projected):
    lengths = jnp.sqrt(jnp.sum(projected * projected, axis=-1, keepdims=True) + norm_eps)
    return (projected / lengths, lengths)


def column_of(row):
    wide = jnp.broadcast_to(row, (128, row.shape[1]))
    return jnp.transpose(wide)[:, :1]


def row_of(column):
    wide = jnp.broadcast_to(column, (column.shape[0], 128))
    return jnp.transpose(wide)[:1, :]


def vmem(megabytes):
    return pltpu.CompilerParams(vmem_limit_bytes=megabytes * 2**20)


def row_block(block, width):
    return pl.BlockSpec((block, width), lambda i: (i, 0))


def lane_block(block):
    return pl.BlockSpec((1, 1, block), lambda i: (i, 0, 0))


def whole(array):
    return pl.BlockSpec(array.shape, lambda i: (0,) * array.ndim)


def stats_kernel(scale, rows_ref, proto_ref, lse_ref):
    logits = jnp.dot(rows_ref[...], proto_ref[...], preferred_element_type=f32)
    peak = jnp.max(logits, axis=-1, keepdims=True)
    total = jnp.sum(jnp.exp2((logits - peak) * scale), axis=-1, keepdims=True)
    lse_ref[0] = row_of(peak * scale + jnp.log2(total))


def local_lse(rows, proto, temp, block):
    count, width = rows.shape
    steps = count // block
    return pl.pallas_call(
        functools.partial(stats_kernel, log2e / temp),
        grid=(steps,),
        in_specs=[row_block(block, width), whole(proto)],
        out_specs=lane_block(block),
        out_shape=jax.ShapeDtypeStruct((steps, 1, block), f32),
        compiler_params=vmem(40),
        cost_estimate=pl.CostEstimate(
            flops=2 * count * proto.size, bytes_accessed=2 * (rows.size + proto.size), transcendentals=count * proto.shape[1]
        ),
    )(rows, proto).reshape(count)


def stored_kernel(scale, rows_ref, proto_ref, peak_ref, lse_ref, powers_ref):
    logits = jnp.dot(rows_ref[...], proto_ref[...], preferred_element_type=f32)
    peak = jnp.max(logits, axis=-1, keepdims=True)
    powers = jnp.exp2((logits - peak) * scale)
    powers_ref[...] = powers.astype(bf16)
    total = jnp.sum(powers, axis=-1, keepdims=True)
    peak_ref[0] = row_of(peak * scale)
    lse_ref[0] = row_of(peak * scale + jnp.log2(total))


def stored_lse(rows, proto, temp, block):
    count, width = rows.shape
    columns = proto.shape[1]
    steps = count // block
    lanes = jax.ShapeDtypeStruct((steps, 1, block), f32)
    peak, lse, powers = pl.pallas_call(
        functools.partial(stored_kernel, log2e / temp),
        grid=(steps,),
        in_specs=[row_block(block, width), whole(proto)],
        out_specs=[lane_block(block), lane_block(block), row_block(block, columns)],
        out_shape=[lanes, lanes, jax.ShapeDtypeStruct((count, columns), bf16)],
        compiler_params=vmem(40),
        cost_estimate=pl.CostEstimate(
            flops=2 * count * proto.size, bytes_accessed=2 * count * columns, transcendentals=count * columns
        ),
    )(rows, proto)
    return peak.reshape(count), lse.reshape(count), powers


def terms_kernel(scale, tile, teacher_ref, lse_ref, powers_s_ref, proto_t_ref, proto_sT_ref, powers_t_ref, terms_s_ref, terms_t_ref):
    teacher = teacher_ref[...]
    lse = column_of(lse_ref[0])
    terms = jnp.zeros(terms_t_ref.shape, f32)
    for start in range(0, proto_t_ref.shape[1], tile):
        cols = slice(start, start + tile)
        logits = jnp.dot(teacher, proto_t_ref[:, cols], preferred_element_type=f32)
        powers = jnp.exp2(logits * scale - lse).astype(bf16)
        powers_t_ref[:, cols] = powers
        terms += jnp.dot(powers, proto_sT_ref[cols, :], preferred_element_type=f32)
    terms_t_ref[...] = terms
    terms_s_ref[...] = jnp.dot(powers_s_ref[...], proto_sT_ref[...], preferred_element_type=f32)


def row_terms(teacher, lse, powers_s, proto_t, proto_sT, temp, block, tile=512):
    count, width = teacher.shape
    columns = proto_t.shape[1]
    steps = count // block
    sums = jax.ShapeDtypeStruct((count, width), f32)
    return pl.pallas_call(
        functools.partial(terms_kernel, log2e / temp, tile),
        grid=(steps,),
        in_specs=[row_block(block, width), lane_block(block), row_block(block, columns), whole(proto_t), whole(proto_sT)],
        out_specs=[row_block(block, columns), row_block(block, width), row_block(block, width)],
        out_shape=[jax.ShapeDtypeStruct((count, columns), bf16), sums, sums],
        compiler_params=vmem(40),
        cost_estimate=pl.CostEstimate(
            flops=6 * count * proto_t.size, bytes_accessed=4 * count * columns, transcendentals=count * columns
        ),
    )(teacher, lse.reshape(steps, 1, block), powers_s, proto_t, proto_sT)


def grads_kernel(tile, student_ref, scale_s_ref, scale_t_ref, powers_s_ref, powers_t_ref, grad_ref):
    @pl.when(pl.program_id(0) == 0)
    def _():
        grad_ref[...] = jnp.zeros_like(grad_ref)

    student_T = jnp.transpose(student_ref[...])
    scale_s, scale_t = column_of(scale_s_ref[0]), column_of(scale_t_ref[0])
    for start in range(0, grad_ref.shape[1], tile):
        cols = slice(start, start + tile)
        grad = scale_s * powers_s_ref[:, cols].astype(f32) - scale_t * powers_t_ref[:, cols].astype(f32)
        grad_ref[:, cols] += jnp.dot(student_T, grad.astype(bf16), preferred_element_type=f32)


def proto_gradient(student, scale_s, scale_t, powers_s, powers_t, block, tile=512):
    count, width = student.shape
    columns = powers_s.shape[1]
    steps = count // block
    return pl.pallas_call(
        functools.partial(grads_kernel, tile),
        grid=(steps,),
        in_specs=[row_block(block, width), lane_block(block), lane_block(block), row_block(block, columns), row_block(block, columns)],
        out_specs=pl.BlockSpec((width, columns), lambda i: (0, 0)),
        out_shape=jax.ShapeDtypeStruct((width, columns), f32),
        compiler_params=vmem(40),
        cost_estimate=pl.CostEstimate(
            flops=2 * count * width * columns, bytes_accessed=4 * count * columns, transcendentals=0
        ),
    )(student, scale_s.reshape(steps, 1, block), scale_t.reshape(steps, 1, block), powers_s, powers_t)


def to_all(block, parts):
    return lax.all_to_all(jnp.broadcast_to(block[None], (parts,) + block.shape), "dp", 0, 0)


def slots_of(counts, capacity):
    lengths = counts + 1
    ends = jnp.cumsum(lengths, axis=-1)
    starts = ends - lengths
    slot = jnp.arange(capacity)[None, :, None]
    inside = (slot >= starts[:, None, :]) & (slot < ends[:, None, :])
    live = jnp.any(inside, axis=-1)
    image = jnp.sum(jnp.where(inside, jnp.arange(counts.shape[1]), 0), axis=-1)
    place = jnp.sum(jnp.where(inside, slot - starts[:, None, :], 0), axis=-1)
    share = jnp.sum(jnp.where(inside, 1.0 / counts.astype(f32)[:, None, :], 0.0), axis=-1)
    return image, place, jnp.where(place == 0, 1.0, share), live


def packed_step(
    teacher_feat,
    teacher_bottleneck,
    teacher_proto,
    student_feat,
    student_bottleneck,
    student_proto,
    mask_index,
    mask_count,
    *,
    parts,
    group,
    capacity,
):
    images, masked = mask_index.shape
    slot_count = masked + 1
    width = student_bottleneck.shape[-1]
    teacher_images = teacher_feat.shape[0]
    teacher_count = teacher_images * slot_count
    padded_count = -(-teacher_count // 8) * 8
    me = lax.axis_index("dp")

    indices = jnp.concatenate([jnp.zeros((images, 1), jnp.int32), mask_index], axis=1)
    first_image = lax.axis_index("group") * teacher_images
    teacher_index = lax.dynamic_slice_in_dim(indices, first_image, teacher_images, 0)
    teacher_rows = teacher_feat[jnp.arange(teacher_images)[:, None], teacher_index].reshape(-1, teacher_feat.shape[-1])
    teacher_unit = normalize_rows(jnp.dot(teacher_rows, teacher_bottleneck, preferred_element_type=f32))[0].astype(bf16)
    teacher_unit = jnp.pad(teacher_unit, ((0, padded_count - teacher_count), (0, 0)))
    member_teacher = to_all(teacher_unit, parts).reshape(-1, width)

    image, place, weight, live = slots_of(mask_count.reshape(parts, images), capacity)
    log_weight = jnp.where(live, jnp.log2(weight / student_temp), -never).reshape(-1)
    mine = lambda array: lax.dynamic_index_in_dim(array, me, 0, keepdims=False)
    my_image, my_place, my_live = mine(image), mine(place), mine(live)
    spread = ((my_image * slot_count + my_place)[:, None] == jnp.arange(images * slot_count)) & my_live[:, None]
    my_rows = jnp.sum(jnp.where(spread, indices.reshape(1, -1), 0), axis=-1)
    source = (image // teacher_images) * padded_count + (image % teacher_images) * slot_count + place
    picks = (source[:, :, None] == jnp.arange(group * padded_count)) & live[:, :, None]

    student_rows = student_feat[my_image, my_rows]
    student_float, lengths = normalize_rows(jnp.dot(student_rows, student_bottleneck, preferred_element_type=f32))
    student_unit = student_float.astype(bf16)
    every_student = to_all(student_unit, parts).reshape(-1, width)

    flip = lambda bit: [(i, i ^ bit) for i in range(group)]
    other_core = lax.ppermute(member_teacher, "group", flip(1))
    other_chip = lax.ppermute(member_teacher, "group", flip(2))
    member_lse = local_lse(member_teacher, teacher_proto, teacher_temp, 256)
    group_lse = lax.all_gather(member_lse, "group", axis=0).reshape(group, parts, padded_count)
    group_lse = group_lse.transpose(1, 0, 2).reshape(parts, 1, group * padded_count)
    lse_t = jnp.sum(jnp.where(picks, group_lse, 0.0), axis=-1).reshape(-1)
    other_chip, every_student, lse_t = lax.optimization_barrier((other_chip, every_student, lse_t))
    far_core = lax.ppermute(other_chip, "group", flip(1))
    held = [array.reshape(parts, padded_count, width) for array in (member_teacher, other_core, other_chip, far_core)]
    held = jnp.concatenate(held, axis=1)
    owner = (image // teacher_images) ^ lax.axis_index("group")
    place_held = owner * padded_count + (image % teacher_images) * slot_count + place
    held_picks = (place_held[:, :, None] == jnp.arange(group * padded_count)) & live[:, :, None]
    every_teacher = lax.dot_general(
        held_picks.astype(bf16), held, (((2,), (1,)), ((0,), (0,))), preferred_element_type=f32
    ).astype(bf16).reshape(-1, width)

    peak_s, lse_s, powers_s = stored_lse(every_student, student_proto, student_temp, 256)
    every_lse = to_all(jnp.concatenate([lse_t, lse_s])[None], parts)
    powers_t, terms_s, terms_t = row_terms(
        every_teacher, lse_t, powers_s, teacher_proto, student_proto.T, teacher_temp, 256
    )
    every_lse, terms_s, terms_t = lax.optimization_barrier((every_lse, terms_s, terms_t))
    top = jnp.max(every_lse, axis=0)
    lse = (top + jnp.log2(jnp.sum(jnp.exp2(every_lse - top), axis=0)))[0]
    rows_total = every_student.shape[0]
    scale_t = jnp.exp2(lse_t - lse[:rows_total] + log_weight)
    scale_s = jnp.exp2(peak_s - lse[rows_total:] + log_weight)
    my_terms = (scale_s[:, None] * terms_s - scale_t[:, None] * terms_t).astype(bf16)
    terms = lax.all_to_all(my_terms.reshape(parts, capacity, width), "dp", 0, 0)
    grad_proto = proto_gradient(every_student, scale_s, scale_t, powers_s, powers_t, 256)
    terms, grad_proto = lax.optimization_barrier((terms, grad_proto))
    feature_grad = jnp.sum(terms.astype(f32), axis=0)
    along_unit = jnp.sum(student_float * feature_grad, axis=-1, keepdims=True)
    unit_grad = ((feature_grad - student_float * along_unit) / lengths).astype(bf16)
    partial_bottleneck = lax.dot_general(
        student_rows, unit_grad, (((0,), (0,)), ((), ())), preferred_element_type=f32
    ).astype(bf16)
    pieces = lax.all_to_all(partial_bottleneck.reshape(parts, -1, width), "dp", 0, 0)
    grad_bottleneck = jnp.sum(pieces.astype(f32), axis=0)
    spread_grad = lax.dot_general(
        spread.astype(bf16), unit_grad, (((0,), (0,)), ((), ())), preferred_element_type=f32
    ).astype(bf16)
    grad_rows = lax.dot_general(
        spread_grad, student_bottleneck, (((1,), (1,)), ((), ())), preferred_element_type=f32
    ).astype(bf16)
    return grad_proto, grad_bottleneck, grad_rows.reshape(images, slot_count, grad_rows.shape[-1])


def on_device(
    teacher_feat,
    teacher_bottleneck,
    teacher_proto,
    student_feat,
    student_bottleneck,
    student_proto,
    mask_index,
    mask_count,
    *,
    parts,
    group,
):
    images, masked = mask_index.shape
    full = images * (masked + 1)
    capacities = [c for c in (104, 112) if c < full] + [full]
    needed = jnp.max(jnp.sum(mask_count.reshape(parts, images) + 1, axis=-1))
    branch = jnp.sum((needed > jnp.array(capacities[:-1])).astype(jnp.int32))
    outs = lax.switch(
        branch,
        [functools.partial(packed_step, parts=parts, group=group, capacity=c) for c in capacities],
        teacher_feat,
        teacher_bottleneck,
        teacher_proto,
        student_feat[0],
        student_bottleneck[0],
        student_proto[0],
        mask_index,
        mask_count,
    )
    return tuple(out[None] for out in outs)


def solution(mesh):
    in_specs = (
        P(("dp", "group"), None, None),
        P(),
        P(None, "dp"),
        P("group", "dp", None, None),
        P("group", None, None),
        P("group", None, "dp"),
        P("dp", None),
        P(),
    )
    out_specs = (P("group", None, "dp"), P("group", "dp", None), P("group", "dp", None, None))
    step = functools.partial(on_device, parts=mesh.shape["dp"], group=mesh.shape["group"])
    return jax.shard_map(step, mesh=mesh, in_specs=in_specs, out_specs=out_specs, check_vma=False)
```

```python
import functools

import jax
import jax.numpy as jnp
from jax import lax
from jax.experimental import pallas as pl
from jax.experimental.pallas import tpu as pltpu
from jax.sharding import PartitionSpec as P

teacher_temp = 0.05
student_temp = 0.1
norm_eps = 1e-06
log2e = 1.4426950408889634
never = 1e30
bf16 = jnp.bfloat16
f32 = jnp.float32


def normalize_rows(projected):
    lengths = jnp.sqrt(jnp.sum(projected * projected, axis=-1, keepdims=True) + norm_eps)
    return (projected / lengths, lengths)


def column_of(row):
    wide = jnp.broadcast_to(row, (128, row.shape[1]))
    return jnp.transpose(wide)[:, :1]


def row_of(column):
    wide = jnp.broadcast_to(column, (column.shape[0], 128))
    return jnp.transpose(wide)[:1, :]


def vmem(megabytes):
    return pltpu.CompilerParams(vmem_limit_bytes=megabytes * 2**20)


def row_block(block, width):
    return pl.BlockSpec((block, width), lambda i: (i, 0))


def lane_block(block):
    return pl.BlockSpec((1, 1, block), lambda i: (i, 0, 0))


def whole(array):
    return pl.BlockSpec(array.shape, lambda i: (0,) * array.ndim)


def times_transposed(left, right):
    return lax.dot_general(left, right, (((1,), (1,)), ((), ())), preferred_element_type=f32)


def powers_of(scale, rows_ref, proto_ref, peak_ref, lse_ref, powers_ref):
    logits = jnp.dot(rows_ref[...], proto_ref[...], preferred_element_type=f32)
    peak = jnp.max(logits, axis=-1, keepdims=True) * scale
    powers = jnp.exp2(logits * scale - peak)
    powers_ref[...] = powers.astype(bf16)
    total = jnp.sum(powers, axis=-1, keepdims=True)
    peak_ref[0] = row_of(peak)
    lse_ref[0] = row_of(peak + jnp.log2(total))


def powers_terms_kernel(scale, rows_ref, proto_ref, peak_ref, lse_ref, powers_ref, terms_ref):
    powers_of(scale, rows_ref, proto_ref, peak_ref, lse_ref, powers_ref)
    terms_ref[...] = times_transposed(powers_ref[...], proto_ref[...]).astype(bf16)


def stored_powers(rows, proto, temp, block, fused):
    count, width = rows.shape
    columns = proto.shape[1]
    steps = count // block
    lanes = jax.ShapeDtypeStruct((steps, 1, block), f32)
    specs = [lane_block(block), lane_block(block), row_block(block, columns), row_block(block, width)]
    shapes = [lanes, lanes, jax.ShapeDtypeStruct((count, columns), bf16), jax.ShapeDtypeStruct((count, width), bf16)]
    peak, lse, *stored = pl.pallas_call(
        functools.partial(powers_terms_kernel if fused else powers_of, log2e / temp),
        grid=(steps,),
        in_specs=[row_block(block, width), whole(proto)],
        out_specs=specs if fused else specs[:3],
        out_shape=shapes if fused else shapes[:3],
        compiler_params=vmem(48),
        cost_estimate=pl.CostEstimate(
            flops=2 * (1 + fused) * count * proto.size, bytes_accessed=2 * count * columns, transcendentals=count * columns
        ),
    )(rows, proto)
    return peak.reshape(count), lse.reshape(count), *stored


def terms_kernel(powers_ref, proto_ref, terms_ref):
    terms_ref[...] = times_transposed(powers_ref[...], proto_ref[...]).astype(bf16)


def row_terms(powers, proto, block):
    count, columns = powers.shape
    width = proto.shape[0]
    return pl.pallas_call(
        terms_kernel,
        grid=(count // block,),
        in_specs=[row_block(block, columns), whole(proto)],
        out_specs=row_block(block, width),
        out_shape=jax.ShapeDtypeStruct((count, width), bf16),
        compiler_params=vmem(48),
        cost_estimate=pl.CostEstimate(flops=2 * count * proto.size, bytes_accessed=2 * count * columns, transcendentals=0),
    )(powers, proto)


def combine_kernel(scale_s_ref, scale_t_ref, terms_s_ref, terms_t_ref, out_ref):
    student = column_of(scale_s_ref[0]) * terms_s_ref[...].astype(f32)
    teacher = column_of(scale_t_ref[0]) * terms_t_ref[...].astype(f32)
    out_ref[...] = (student - teacher).astype(bf16)


def combined_terms(scale_s, scale_t, terms_s, terms_t, block):
    count, width = terms_s.shape
    steps = count // block
    return pl.pallas_call(
        combine_kernel,
        grid=(steps,),
        in_specs=[lane_block(block), lane_block(block), row_block(block, width), row_block(block, width)],
        out_specs=row_block(block, width),
        out_shape=jax.ShapeDtypeStruct((count, width), bf16),
        compiler_params=vmem(24),
        cost_estimate=pl.CostEstimate(flops=3 * count * width, bytes_accessed=6 * count * width, transcendentals=0),
    )(scale_s.reshape(steps, 1, block), scale_t.reshape(steps, 1, block), terms_s, terms_t)


def grads_kernel(tile, student_ref, scale_s_ref, scale_t_ref, powers_s_ref, powers_t_ref, grad_ref):
    @pl.when(pl.program_id(0) == 0)
    def _():
        grad_ref[...] = jnp.zeros_like(grad_ref)

    student_T = jnp.transpose(student_ref[...])
    scale_s, scale_t = column_of(scale_s_ref[0]), column_of(scale_t_ref[0])
    for start in range(0, grad_ref.shape[1], tile):
        cols = slice(start, start + tile)
        grad = scale_s * powers_s_ref[:, cols].astype(f32) - scale_t * powers_t_ref[:, cols].astype(f32)
        grad_ref[:, cols] += jnp.dot(student_T, grad.astype(bf16), preferred_element_type=f32)


def proto_gradient(student, scale_s, scale_t, powers_s, powers_t, block, tile=512):
    count, width = student.shape
    columns = powers_s.shape[1]
    steps = count // block
    return pl.pallas_call(
        functools.partial(grads_kernel, tile),
        grid=(steps,),
        in_specs=[row_block(block, width), lane_block(block), lane_block(block), row_block(block, columns), row_block(block, columns)],
        out_specs=pl.BlockSpec((width, columns), lambda i: (0, 0)),
        out_shape=jax.ShapeDtypeStruct((width, columns), f32),
        compiler_params=vmem(48),
        cost_estimate=pl.CostEstimate(
            flops=2 * count * width * columns, bytes_accessed=4 * count * columns, transcendentals=0
        ),
    )(student, scale_s.reshape(steps, 1, block), scale_t.reshape(steps, 1, block), powers_s, powers_t)


def to_all(block, parts):
    return lax.all_to_all(jnp.broadcast_to(block[None], (parts,) + block.shape), "dp", 0, 0)


def slots_of(counts, capacity):
    lengths = counts + 1
    ends = jnp.cumsum(lengths, axis=-1)
    starts = ends - lengths
    slot = jnp.arange(capacity)[None, :, None]
    inside = (slot >= starts[:, None, :]) & (slot < ends[:, None, :])
    live = jnp.any(inside, axis=-1)
    image = jnp.sum(jnp.where(inside, jnp.arange(counts.shape[1]), 0), axis=-1)
    place = jnp.sum(jnp.where(inside, slot - starts[:, None, :], 0), axis=-1)
    share = jnp.sum(jnp.where(inside, 1.0 / counts.astype(f32)[:, None, :], 0.0), axis=-1)
    return image, place, jnp.where(place == 0, 1.0, share), live


def packed_step(
    teacher_feat,
    teacher_bottleneck,
    teacher_proto,
    student_feat,
    student_bottleneck,
    student_proto,
    mask_index,
    mask_count,
    *,
    parts,
    capacity,
):
    images, masked = mask_index.shape
    slot_count = masked + 1
    width = student_bottleneck.shape[-1]
    teacher_images = teacher_feat.shape[0]
    block = 8 * capacity
    me = lax.axis_index("dp")
    indices = jnp.concatenate([jnp.zeros((images, 1), jnp.int32), mask_index], axis=1)

    image, place, weight, live = slots_of(mask_count.reshape(parts, images), capacity)
    log_weight = jnp.where(live, jnp.log2(weight / student_temp), -never).reshape(-1)
    mine = lambda array: lax.dynamic_index_in_dim(array, me, 0, keepdims=False)
    my_image, my_place, my_live = mine(image), mine(place), mine(live)
    spread = ((my_image * slot_count + my_place)[:, None] == jnp.arange(images * slot_count)) & my_live[:, None]
    my_rows = jnp.sum(jnp.where(spread, indices.reshape(1, -1), 0), axis=-1)
    spread = spread.astype(bf16)

    student_rows = student_feat[my_image, my_rows]
    student_float, lengths = normalize_rows(jnp.dot(student_rows, student_bottleneck, preferred_element_type=f32))
    student_unit = student_float.astype(bf16)
    every_student = to_all(student_unit, parts).reshape(-1, width)

    first_image = lax.axis_index("group") * teacher_images
    teacher_index = lax.dynamic_slice_in_dim(indices, first_image, teacher_images, 0)
    teacher_rows = teacher_feat[jnp.arange(teacher_images)[:, None], teacher_index].reshape(-1, teacher_feat.shape[-1])
    teacher_unit = normalize_rows(jnp.dot(teacher_rows, teacher_bottleneck, preferred_element_type=f32))[0].astype(bf16)
    group_teacher = lax.all_gather(teacher_unit, "group", axis=0, tiled=True)
    group_teacher = jnp.dot(spread, group_teacher, preferred_element_type=f32).astype(bf16)
    group_teacher, every_student = lax.optimization_barrier((group_teacher, every_student))
    every_teacher = to_all(group_teacher, parts).reshape(-1, width)

    peak_s, lse_s, powers_s, terms_s = stored_powers(every_student, student_proto, student_temp, block, True)
    every_teacher, terms_s = lax.optimization_barrier((every_teacher, terms_s))
    peak_t, lse_t, powers_t = stored_powers(every_teacher, teacher_proto, teacher_temp, block, False)
    every_lse = to_all(jnp.concatenate([lse_t, lse_s])[None], parts)
    terms_t = row_terms(powers_t, student_proto, block)
    every_lse, terms_t = lax.optimization_barrier((every_lse, terms_t))
    top = jnp.max(every_lse, axis=0)
    lse = (top + jnp.log2(jnp.sum(jnp.exp2(every_lse - top), axis=0)))[0]
    rows_total = every_student.shape[0]
    scale_t = jnp.exp2(peak_t - lse[:rows_total] + log_weight)
    scale_s = jnp.exp2(peak_s - lse[rows_total:] + log_weight)
    my_terms = combined_terms(scale_s, scale_t, terms_s, terms_t, block)
    terms = lax.all_to_all(my_terms.reshape(parts, capacity, width), "dp", 0, 0)
    grad_proto = proto_gradient(every_student, scale_s, scale_t, powers_s, powers_t, block)
    terms, grad_proto = lax.optimization_barrier((terms, grad_proto))
    feature_grad = jnp.sum(terms.astype(f32), axis=0)
    along_unit = jnp.sum(student_float * feature_grad, axis=-1, keepdims=True)
    unit_grad = ((feature_grad - student_float * along_unit) / lengths).astype(bf16)
    partial_bottleneck = lax.dot_general(
        student_rows, unit_grad, (((0,), (0,)), ((), ())), preferred_element_type=f32
    ).astype(bf16)
    pieces = lax.all_to_all(partial_bottleneck.reshape(parts, -1, width), "dp", 0, 0)
    grad_bottleneck = jnp.sum(pieces.astype(f32), axis=0)
    spread_grad = lax.dot_general(
        spread, unit_grad, (((0,), (0,)), ((), ())), preferred_element_type=f32
    ).astype(bf16)
    grad_rows = lax.dot_general(
        spread_grad, student_bottleneck, (((1,), (1,)), ((), ())), preferred_element_type=f32
    ).astype(bf16)
    return grad_proto, grad_bottleneck, grad_rows.reshape(images, slot_count, grad_rows.shape[-1])


def on_device(
    teacher_feat,
    teacher_bottleneck,
    teacher_proto,
    student_feat,
    student_bottleneck,
    student_proto,
    mask_index,
    mask_count,
    *,
    parts,
):
    images, masked = mask_index.shape
    full = images * (masked + 1)
    capacities = [c for c in (104, 112) if c < full] + [full]
    needed = jnp.max(jnp.sum(mask_count.reshape(parts, images) + 1, axis=-1))
    branch = sum((needed > c).astype(jnp.int32) for c in capacities[:-1])
    outs = lax.switch(
        branch,
        [functools.partial(packed_step, parts=parts, capacity=c) for c in capacities],
        teacher_feat,
        teacher_bottleneck,
        teacher_proto,
        student_feat[0],
        student_bottleneck[0],
        student_proto[0],
        mask_index,
        mask_count,
    )
    return tuple(out[None] for out in outs)


def solution(mesh):
    in_specs = (
        P(("dp", "group"), None, None),
        P(),
        P(None, "dp"),
        P("group", "dp", None, None),
        P("group", None, None),
        P("group", None, "dp"),
        P("dp", None),
        P(),
    )
    out_specs = (P("group", None, "dp"), P("group", "dp", None), P("group", "dp", None, None))
    step = functools.partial(on_device, parts=mesh.shape["dp"])
    return jax.shard_map(step, mesh=mesh, in_specs=in_specs, out_specs=out_specs, check_vma=False)
```

```python
import functools

import jax
import jax.numpy as jnp
from jax import lax
from jax.experimental import pallas as pl
from jax.experimental.pallas import tpu as pltpu
from jax.sharding import PartitionSpec as P

teacher_temp = 0.05
student_temp = 0.1
norm_eps = 1e-06
log2e = 1.4426950408889634
never = 1e30
bf16 = jnp.bfloat16
f32 = jnp.float32


def normalize_rows(projected):
    lengths = jnp.sqrt(jnp.sum(projected * projected, axis=-1, keepdims=True) + norm_eps)
    return (projected / lengths, lengths)


def column_of(row):
    wide = jnp.broadcast_to(row, (128, row.shape[1]))
    return jnp.transpose(wide)[:, :1]


def row_of(column):
    wide = jnp.broadcast_to(column, (column.shape[0], 128))
    return jnp.transpose(wide)[:1, :]


def vmem(megabytes):
    return pltpu.CompilerParams(vmem_limit_bytes=megabytes * 2**20)


def row_block(block, width):
    return pl.BlockSpec((block, width), lambda i: (i, 0))


def lane_block(block):
    return pl.BlockSpec((1, 1, block), lambda i: (i, 0, 0))


def whole(array):
    return pl.BlockSpec(array.shape, lambda i: (0,) * array.ndim)


def times_transposed(left, right):
    return lax.dot_general(left, right, (((1,), (1,)), ((), ())), preferred_element_type=f32)


def powers_of(scale, rows_ref, proto_ref, peak_ref, lse_ref, powers_ref):
    logits = jnp.dot(rows_ref[...], proto_ref[...], preferred_element_type=f32)
    peak = jnp.max(logits, axis=-1, keepdims=True) * scale
    powers = jnp.exp2(logits * scale - peak)
    powers_ref[...] = powers.astype(bf16)
    total = jnp.sum(powers, axis=-1, keepdims=True)
    peak_ref[0] = row_of(peak)
    lse_ref[0] = row_of(peak + jnp.log2(total))


def powers_terms_kernel(scale, rows_ref, proto_ref, peak_ref, lse_ref, powers_ref, terms_ref):
    powers_of(scale, rows_ref, proto_ref, peak_ref, lse_ref, powers_ref)
    terms_ref[...] = times_transposed(powers_ref[...], proto_ref[...]).astype(bf16)


def stored_powers(rows, proto, temp, block, fused):
    count, width = rows.shape
    columns = proto.shape[1]
    steps = count // block
    lanes = jax.ShapeDtypeStruct((steps, 1, block), f32)
    specs = [lane_block(block), lane_block(block), row_block(block, columns), row_block(block, width)]
    shapes = [lanes, lanes, jax.ShapeDtypeStruct((count, columns), bf16), jax.ShapeDtypeStruct((count, width), bf16)]
    peak, lse, *stored = pl.pallas_call(
        functools.partial(powers_terms_kernel if fused else powers_of, log2e / temp),
        grid=(steps,),
        in_specs=[row_block(block, width), whole(proto)],
        out_specs=specs if fused else specs[:3],
        out_shape=shapes if fused else shapes[:3],
        compiler_params=vmem(48),
        cost_estimate=pl.CostEstimate(
            flops=2 * (1 + fused) * count * proto.size, bytes_accessed=2 * count * columns, transcendentals=count * columns
        ),
    )(rows, proto)
    return peak.reshape(count), lse.reshape(count), *stored


def terms_kernel(powers_ref, proto_ref, terms_ref):
    terms_ref[...] = times_transposed(powers_ref[...], proto_ref[...]).astype(bf16)


def row_terms(powers, proto, block):
    count, columns = powers.shape
    width = proto.shape[0]
    return pl.pallas_call(
        terms_kernel,
        grid=(count // block,),
        in_specs=[row_block(block, columns), whole(proto)],
        out_specs=row_block(block, width),
        out_shape=jax.ShapeDtypeStruct((count, width), bf16),
        compiler_params=vmem(48),
        cost_estimate=pl.CostEstimate(flops=2 * count * proto.size, bytes_accessed=2 * count * columns, transcendentals=0),
    )(powers, proto)


def combine_kernel(scale_s_ref, scale_t_ref, terms_s_ref, terms_t_ref, out_ref):
    student = column_of(scale_s_ref[0]) * terms_s_ref[...].astype(f32)
    teacher = column_of(scale_t_ref[0]) * terms_t_ref[...].astype(f32)
    out_ref[...] = (student - teacher).astype(bf16)


def combined_terms(scale_s, scale_t, terms_s, terms_t, block):
    count, width = terms_s.shape
    steps = count // block
    return pl.pallas_call(
        combine_kernel,
        grid=(steps,),
        in_specs=[lane_block(block), lane_block(block), row_block(block, width), row_block(block, width)],
        out_specs=row_block(block, width),
        out_shape=jax.ShapeDtypeStruct((count, width), bf16),
        compiler_params=vmem(24),
        cost_estimate=pl.CostEstimate(flops=3 * count * width, bytes_accessed=6 * count * width, transcendentals=0),
    )(scale_s.reshape(steps, 1, block), scale_t.reshape(steps, 1, block), terms_s, terms_t)


def grads_kernel(tile, student_ref, scale_s_ref, scale_t_ref, powers_s_ref, powers_t_ref, grad_ref):
    @pl.when(pl.program_id(0) == 0)
    def _():
        grad_ref[...] = jnp.zeros_like(grad_ref)

    student_T = jnp.transpose(student_ref[...])
    scale_s, scale_t = column_of(scale_s_ref[0]), column_of(scale_t_ref[0])
    for start in range(0, grad_ref.shape[1], tile):
        cols = slice(start, start + tile)
        grad = scale_s * powers_s_ref[:, cols].astype(f32) - scale_t * powers_t_ref[:, cols].astype(f32)
        grad_ref[:, cols] += jnp.dot(student_T, grad.astype(bf16), preferred_element_type=f32)


def proto_gradient(student, scale_s, scale_t, powers_s, powers_t, block, tile=512):
    count, width = student.shape
    columns = powers_s.shape[1]
    steps = count // block
    return pl.pallas_call(
        functools.partial(grads_kernel, tile),
        grid=(steps,),
        in_specs=[row_block(block, width), lane_block(block), lane_block(block), row_block(block, columns), row_block(block, columns)],
        out_specs=pl.BlockSpec((width, columns), lambda i: (0, 0)),
        out_shape=jax.ShapeDtypeStruct((width, columns), f32),
        compiler_params=vmem(48),
        cost_estimate=pl.CostEstimate(
            flops=2 * count * width * columns, bytes_accessed=4 * count * columns, transcendentals=0
        ),
    )(student, scale_s.reshape(steps, 1, block), scale_t.reshape(steps, 1, block), powers_s, powers_t)


def to_all(block, parts):
    return lax.all_to_all(jnp.broadcast_to(block[None], (parts,) + block.shape), "dp", 0, 0)


def slots_of(counts, capacity):
    lengths = counts + 1
    ends = jnp.cumsum(lengths, axis=-1)
    starts = ends - lengths
    slot = jnp.arange(capacity)[None, :, None]
    inside = (slot >= starts[:, None, :]) & (slot < ends[:, None, :])
    live = jnp.any(inside, axis=-1)
    image = jnp.sum(jnp.where(inside, jnp.arange(counts.shape[1]), 0), axis=-1)
    place = jnp.sum(jnp.where(inside, slot - starts[:, None, :], 0), axis=-1)
    share = jnp.sum(jnp.where(inside, 1.0 / counts.astype(f32)[:, None, :], 0.0), axis=-1)
    return image, place, jnp.where(place == 0, 1.0, share), live


def packed_step(
    teacher_feat,
    teacher_bottleneck,
    teacher_proto,
    student_feat,
    student_bottleneck,
    student_proto,
    mask_index,
    mask_count,
    *,
    parts,
    group,
    capacity,
):
    images, masked = mask_index.shape
    slot_count = masked + 1
    width = student_bottleneck.shape[-1]
    teacher_images = teacher_feat.shape[0]
    teacher_count = teacher_images * slot_count
    padded_count = -(-teacher_count // 16) * 16
    block = 8 * capacity if capacity < 110 else 4 * capacity if capacity < 120 else 256
    me = lax.axis_index("dp")
    indices = jnp.concatenate([jnp.zeros((images, 1), jnp.int32), mask_index], axis=1)

    image, place, weight, live = slots_of(mask_count.reshape(parts, images), capacity)
    log_weight = jnp.where(live, jnp.log2(weight / student_temp), -never).reshape(-1)
    mine = lambda array: lax.dynamic_index_in_dim(array, me, 0, keepdims=False)
    my_image, my_place, my_live = mine(image), mine(place), mine(live)
    spread = ((my_image * slot_count + my_place)[:, None] == jnp.arange(images * slot_count)) & my_live[:, None]
    my_rows = jnp.sum(jnp.where(spread, indices.reshape(1, -1), 0), axis=-1)
    spread = spread.astype(bf16)

    student_rows = student_feat[my_image, my_rows]
    student_float, lengths = normalize_rows(jnp.dot(student_rows, student_bottleneck, preferred_element_type=f32))
    student_unit = student_float.astype(bf16)
    every_student = to_all(student_unit, parts).reshape(-1, width)

    first_image = lax.axis_index("group") * teacher_images
    teacher_index = lax.dynamic_slice_in_dim(indices, first_image, teacher_images, 0)
    teacher_rows = teacher_feat[jnp.arange(teacher_images)[:, None], teacher_index].reshape(-1, teacher_feat.shape[-1])
    teacher_unit = normalize_rows(jnp.dot(teacher_rows, teacher_bottleneck, preferred_element_type=f32))[0].astype(bf16)
    teacher_unit = jnp.pad(teacher_unit, ((0, padded_count - teacher_count), (0, 0)))
    others = [lax.ppermute(teacher_unit, "group", [(i, i ^ k) for i in range(group)]) for k in range(1, group)]
    group_teacher = jnp.concatenate([teacher_unit] + others)
    owner = (my_image // teacher_images) ^ lax.axis_index("group")
    held = owner * padded_count + (my_image % teacher_images) * slot_count + my_place
    picks = ((held[:, None] == jnp.arange(group * padded_count)) & my_live[:, None]).astype(bf16)
    group_teacher = jnp.dot(picks, group_teacher, preferred_element_type=f32).astype(bf16)
    group_teacher, every_student = lax.optimization_barrier((group_teacher, every_student))
    every_teacher = to_all(group_teacher, parts).reshape(-1, width)

    peak_s, lse_s, powers_s, terms_s = stored_powers(every_student, student_proto, student_temp, block, True)
    every_teacher, terms_s = lax.optimization_barrier((every_teacher, terms_s))
    peak_t, lse_t, powers_t = stored_powers(every_teacher, teacher_proto, teacher_temp, block, False)
    every_lse = to_all(jnp.concatenate([lse_t, lse_s])[None], parts)
    terms_t = row_terms(powers_t, student_proto, block)
    every_lse, terms_t = lax.optimization_barrier((every_lse, terms_t))
    top = jnp.max(every_lse, axis=0)
    lse = (top + jnp.log2(jnp.sum(jnp.exp2(every_lse - top), axis=0)))[0]
    rows_total = every_student.shape[0]
    scale_t = jnp.exp2(peak_t - lse[:rows_total] + log_weight)
    scale_s = jnp.exp2(peak_s - lse[rows_total:] + log_weight)
    my_terms = combined_terms(scale_s, scale_t, terms_s, terms_t, block)
    terms = lax.all_to_all(my_terms.reshape(parts, capacity, width), "dp", 0, 0)
    grad_proto = proto_gradient(every_student, scale_s, scale_t, powers_s, powers_t, block)
    terms, grad_proto = lax.optimization_barrier((terms, grad_proto))
    feature_grad = jnp.sum(terms.astype(f32), axis=0)
    along_unit = jnp.sum(student_float * feature_grad, axis=-1, keepdims=True)
    unit_grad = ((feature_grad - student_float * along_unit) / lengths).astype(bf16)
    partial_bottleneck = lax.dot_general(
        student_rows, unit_grad, (((0,), (0,)), ((), ())), preferred_element_type=f32
    ).astype(bf16)
    pieces = lax.all_to_all(partial_bottleneck.reshape(parts, -1, width), "dp", 0, 0)
    grad_bottleneck = jnp.sum(pieces.astype(f32), axis=0)
    spread_grad = lax.dot_general(
        spread, unit_grad, (((0,), (0,)), ((), ())), preferred_element_type=f32
    ).astype(bf16)
    grad_rows = lax.dot_general(
        spread_grad, student_bottleneck, (((1,), (1,)), ((), ())), preferred_element_type=f32
    ).astype(bf16)
    return grad_proto, grad_bottleneck, grad_rows.reshape(images, slot_count, grad_rows.shape[-1])


def on_device(
    teacher_feat,
    teacher_bottleneck,
    teacher_proto,
    student_feat,
    student_bottleneck,
    student_proto,
    mask_index,
    mask_count,
    *,
    parts,
    group,
):
    images, masked = mask_index.shape
    full = images * (masked + 1)
    capacities = [c for c in (104, 112) if c < full] + [full]
    needed = jnp.max(jnp.sum(mask_count.reshape(parts, images) + 1, axis=-1))
    branch = sum((needed > c).astype(jnp.int32) for c in capacities[:-1])
    outs = lax.switch(
        branch,
        [functools.partial(packed_step, parts=parts, group=group, capacity=c) for c in capacities],
        teacher_feat,
        teacher_bottleneck,
        teacher_proto,
        student_feat[0],
        student_bottleneck[0],
        student_proto[0],
        mask_index,
        mask_count,
    )
    return tuple(out[None] for out in outs)


def solution(mesh):
    in_specs = (
        P(("dp", "group"), None, None),
        P(),
        P(None, "dp"),
        P("group", "dp", None, None),
        P("group", None, None),
        P("group", None, "dp"),
        P("dp", None),
        P(),
    )
    out_specs = (P("group", None, "dp"), P("group", "dp", None), P("group", "dp", None, None))
    step = functools.partial(on_device, parts=mesh.shape["dp"], group=mesh.shape["group"])
    return jax.shard_map(step, mesh=mesh, in_specs=in_specs, out_specs=out_specs, check_vma=False)
```

```python
import functools

import jax
import jax.numpy as jnp
from jax import lax
from jax.experimental import pallas as pl
from jax.experimental.pallas import tpu as pltpu
from jax.sharding import PartitionSpec as P

teacher_temp = 0.05
student_temp = 0.1
norm_eps = 1e-06
log2e = 1.4426950408889634
never = 1e30
bf16 = jnp.bfloat16
f32 = jnp.float32


def normalize_rows(projected):
    lengths = jnp.sqrt(jnp.sum(projected * projected, axis=-1, keepdims=True) + norm_eps)
    return (projected / lengths, lengths)


def column_of(row):
    wide = jnp.broadcast_to(row, (128, row.shape[1]))
    return jnp.transpose(wide)[:, :1]


def row_of(column):
    wide = jnp.broadcast_to(column, (column.shape[0], 128))
    return jnp.transpose(wide)[:1, :]


def vmem(megabytes):
    return pltpu.CompilerParams(vmem_limit_bytes=megabytes * 2**20)


def row_block(block, width):
    return pl.BlockSpec((block, width), lambda i: (i, 0))


def lane_block(block):
    return pl.BlockSpec((1, 1, block), lambda i: (i, 0, 0))


def whole(array):
    return pl.BlockSpec(array.shape, lambda i: (0,) * array.ndim)


def times_transposed(left, right):
    return lax.dot_general(left, right, (((1,), (1,)), ((), ())), preferred_element_type=f32)


def powers_of(scale, rows_ref, proto_ref, peak_ref, lse_ref, powers_ref):
    logits = jnp.dot(rows_ref[...], proto_ref[...], preferred_element_type=f32)
    peak = jnp.max(logits, axis=-1, keepdims=True) * scale
    powers = jnp.exp2(logits * scale - peak)
    powers_ref[...] = powers.astype(bf16)
    total = jnp.sum(powers, axis=-1, keepdims=True)
    peak_ref[0] = row_of(peak)
    lse_ref[0] = row_of(peak + jnp.log2(total))


def powers_terms_kernel(scale, rows_ref, proto_ref, peak_ref, lse_ref, powers_ref, terms_ref):
    powers_of(scale, rows_ref, proto_ref, peak_ref, lse_ref, powers_ref)
    terms_ref[...] = times_transposed(powers_ref[...], proto_ref[...]).astype(bf16)


def stored_powers(rows, proto, temp, block, fused):
    count, width = rows.shape
    columns = proto.shape[1]
    steps = count // block
    lanes = jax.ShapeDtypeStruct((steps, 1, block), f32)
    specs = [lane_block(block), lane_block(block), row_block(block, columns), row_block(block, width)]
    shapes = [lanes, lanes, jax.ShapeDtypeStruct((count, columns), bf16), jax.ShapeDtypeStruct((count, width), bf16)]
    peak, lse, *stored = pl.pallas_call(
        functools.partial(powers_terms_kernel if fused else powers_of, log2e / temp),
        grid=(steps,),
        in_specs=[row_block(block, width), whole(proto)],
        out_specs=specs if fused else specs[:3],
        out_shape=shapes if fused else shapes[:3],
        compiler_params=vmem(48),
        cost_estimate=pl.CostEstimate(
            flops=2 * (1 + fused) * count * proto.size, bytes_accessed=2 * count * columns, transcendentals=count * columns
        ),
    )(rows, proto)
    return peak, lse, *stored


def terms_kernel(powers_ref, proto_ref, terms_ref):
    terms_ref[...] = times_transposed(powers_ref[...], proto_ref[...]).astype(bf16)


def row_terms(powers, proto, block):
    count, columns = powers.shape
    width = proto.shape[0]
    return pl.pallas_call(
        terms_kernel,
        grid=(count // block,),
        in_specs=[row_block(block, columns), whole(proto)],
        out_specs=row_block(block, width),
        out_shape=jax.ShapeDtypeStruct((count, width), bf16),
        compiler_params=vmem(48),
        cost_estimate=pl.CostEstimate(flops=2 * count * proto.size, bytes_accessed=2 * count * columns, transcendentals=0),
    )(powers, proto)


def total_lse(parts_lse):
    top = jnp.max(parts_lse, axis=0)
    return top + jnp.log2(jnp.sum(jnp.exp2(parts_lse - top), axis=0))


def combine_kernel(lse_s_ref, lse_t_ref, peak_s_ref, peak_t_ref, weight_ref, terms_s_ref, terms_t_ref,
                   out_ref, scale_s_ref, scale_t_ref):
    scale_s = jnp.exp2(peak_s_ref[0] - total_lse(lse_s_ref[:, 0]) + weight_ref[0])
    scale_t = jnp.exp2(peak_t_ref[0] - total_lse(lse_t_ref[:, 0]) + weight_ref[0])
    scale_s_ref[0] = scale_s
    scale_t_ref[0] = scale_t
    student = column_of(scale_s) * terms_s_ref[...].astype(f32)
    teacher = column_of(scale_t) * terms_t_ref[...].astype(f32)
    out_ref[...] = (student - teacher).astype(bf16)


def combined_terms(every_lse, peak_s, peak_t, log_weight, terms_s, terms_t):
    count, width = terms_s.shape
    steps, _, block = peak_s.shape
    parts = every_lse.shape[0]
    lanes = jax.ShapeDtypeStruct(peak_s.shape, f32)
    return pl.pallas_call(
        combine_kernel,
        grid=(steps,),
        in_specs=[
            pl.BlockSpec((parts, 1, 1, block), lambda i: (0, i, 0, 0)),
            pl.BlockSpec((parts, 1, 1, block), lambda i: (0, i + steps, 0, 0)),
            lane_block(block),
            lane_block(block),
            lane_block(block),
            row_block(block, width),
            row_block(block, width),
        ],
        out_specs=[row_block(block, width), lane_block(block), lane_block(block)],
        out_shape=[jax.ShapeDtypeStruct((count, width), bf16), lanes, lanes],
        compiler_params=vmem(24),
        cost_estimate=pl.CostEstimate(flops=3 * count * width, bytes_accessed=6 * count * width, transcendentals=64 * count),
    )(every_lse, every_lse, peak_s, peak_t, log_weight, terms_s, terms_t)


def grads_kernel(tile, student_ref, scale_s_ref, scale_t_ref, powers_s_ref, powers_t_ref, grad_ref):
    @pl.when(pl.program_id(0) == 0)
    def _():
        grad_ref[...] = jnp.zeros_like(grad_ref)

    student_T = jnp.transpose(student_ref[...])
    scale_s, scale_t = column_of(scale_s_ref[0]), column_of(scale_t_ref[0])
    for start in range(0, grad_ref.shape[1], tile):
        cols = slice(start, start + tile)
        grad = scale_s * powers_s_ref[:, cols].astype(f32) - scale_t * powers_t_ref[:, cols].astype(f32)
        grad_ref[:, cols] += jnp.dot(student_T, grad.astype(bf16), preferred_element_type=f32)


def proto_gradient(student, scale_s, scale_t, powers_s, powers_t, block, tile=512):
    count, width = student.shape
    columns = powers_s.shape[1]
    steps = count // block
    return pl.pallas_call(
        functools.partial(grads_kernel, tile),
        grid=(steps,),
        in_specs=[row_block(block, width), lane_block(block), lane_block(block), row_block(block, columns), row_block(block, columns)],
        out_specs=pl.BlockSpec((width, columns), lambda i: (0, 0)),
        out_shape=jax.ShapeDtypeStruct((width, columns), f32),
        compiler_params=vmem(48),
        cost_estimate=pl.CostEstimate(
            flops=2 * count * width * columns, bytes_accessed=4 * count * columns, transcendentals=0
        ),
    )(student, scale_s, scale_t, powers_s, powers_t)


def to_all(block, parts):
    return lax.all_to_all(jnp.broadcast_to(block[None], (parts,) + block.shape), "dp", 0, 0)


def slots_of(counts, capacity):
    lengths = counts + 1
    ends = jnp.cumsum(lengths, axis=-1)
    starts = ends - lengths
    slot = jnp.arange(capacity)[None, :, None]
    inside = (slot >= starts[:, None, :]) & (slot < ends[:, None, :])
    live = jnp.any(inside, axis=-1)
    image = jnp.sum(jnp.where(inside, jnp.arange(counts.shape[1]), 0), axis=-1)
    place = jnp.sum(jnp.where(inside, slot - starts[:, None, :], 0), axis=-1)
    share = jnp.sum(jnp.where(inside, 1.0 / counts.astype(f32)[:, None, :], 0.0), axis=-1)
    return image, place, jnp.where(place == 0, 1.0, share), live


def packed_step(
    teacher_feat,
    teacher_bottleneck,
    teacher_proto,
    student_feat,
    student_bottleneck,
    student_proto,
    mask_index,
    mask_count,
    *,
    parts,
    group,
    capacity,
):
    images, masked = mask_index.shape
    slot_count = masked + 1
    width = student_bottleneck.shape[-1]
    teacher_images = teacher_feat.shape[0]
    teacher_count = teacher_images * slot_count
    padded_count = -(-teacher_count // 16) * 16
    block = 8 * capacity if capacity < 110 else 4 * capacity if capacity < 120 else 256
    me = lax.axis_index("dp")
    indices = jnp.concatenate([jnp.zeros((images, 1), jnp.int32), mask_index], axis=1)

    image, place, weight, live = slots_of(mask_count.reshape(parts, images), capacity)
    log_weight = jnp.where(live, jnp.log2(weight / student_temp), -never).reshape(-1)
    mine = lambda array: lax.dynamic_index_in_dim(array, me, 0, keepdims=False)
    my_image, my_place, my_live = mine(image), mine(place), mine(live)
    spread = ((my_image * slot_count + my_place)[:, None] == jnp.arange(images * slot_count)) & my_live[:, None]
    my_rows = jnp.sum(jnp.where(spread, indices.reshape(1, -1), 0), axis=-1)
    spread = spread.astype(bf16)

    student_rows = student_feat[my_image, my_rows]
    student_float, lengths = normalize_rows(jnp.dot(student_rows, student_bottleneck, preferred_element_type=f32))
    student_unit = student_float.astype(bf16)
    every_student = to_all(student_unit, parts).reshape(-1, width)

    first_image = lax.axis_index("group") * teacher_images
    teacher_index = lax.dynamic_slice_in_dim(indices, first_image, teacher_images, 0)
    teacher_rows = teacher_feat[jnp.arange(teacher_images)[:, None], teacher_index].reshape(-1, teacher_feat.shape[-1])
    teacher_unit = normalize_rows(jnp.dot(teacher_rows, teacher_bottleneck, preferred_element_type=f32))[0].astype(bf16)
    teacher_unit = jnp.pad(teacher_unit, ((0, padded_count - teacher_count), (0, 0)))
    others = [lax.ppermute(teacher_unit, "group", [(i, i ^ k) for i in range(group)]) for k in range(1, group)]
    group_teacher = jnp.concatenate([teacher_unit] + others)
    owner = (my_image // teacher_images) ^ lax.axis_index("group")
    held = owner * padded_count + (my_image % teacher_images) * slot_count + my_place
    picks = ((held[:, None] == jnp.arange(group * padded_count)) & my_live[:, None]).astype(bf16)
    group_teacher = jnp.dot(picks, group_teacher, preferred_element_type=f32).astype(bf16)
    group_teacher, every_student = lax.optimization_barrier((group_teacher, every_student))
    every_teacher = to_all(group_teacher, parts).reshape(-1, width)

    peak_s, lse_s, powers_s, terms_s = stored_powers(every_student, student_proto, student_temp, block, True)
    every_teacher, terms_s = lax.optimization_barrier((every_teacher, terms_s))
    peak_t, lse_t, powers_t = stored_powers(every_teacher, teacher_proto, teacher_temp, block, False)
    every_lse = to_all(jnp.concatenate([lse_s, lse_t]), parts)
    terms_t = row_terms(powers_t, student_proto, block)
    every_lse, terms_t = lax.optimization_barrier((every_lse, terms_t))
    my_terms, scale_s, scale_t = combined_terms(
        every_lse, peak_s, peak_t, log_weight.reshape(peak_s.shape), terms_s, terms_t
    )
    terms = lax.all_to_all(my_terms.reshape(parts, capacity, width), "dp", 0, 0)
    grad_proto = proto_gradient(every_student, scale_s, scale_t, powers_s, powers_t, block)
    terms, grad_proto = lax.optimization_barrier((terms, grad_proto))
    feature_grad = jnp.sum(terms.astype(f32), axis=0)
    along_unit = jnp.sum(student_float * feature_grad, axis=-1, keepdims=True)
    unit_grad = ((feature_grad - student_float * along_unit) / lengths).astype(bf16)
    partial_bottleneck = lax.dot_general(
        student_rows, unit_grad, (((0,), (0,)), ((), ())), preferred_element_type=f32
    ).astype(bf16)
    pieces = lax.all_to_all(partial_bottleneck.reshape(parts, -1, width), "dp", 0, 0)
    grad_bottleneck = jnp.sum(pieces.astype(f32), axis=0)
    spread_grad = lax.dot_general(
        spread, unit_grad, (((0,), (0,)), ((), ())), preferred_element_type=f32
    ).astype(bf16)
    grad_rows = lax.dot_general(
        spread_grad, student_bottleneck, (((1,), (1,)), ((), ())), preferred_element_type=f32
    ).astype(bf16)
    return grad_proto, grad_bottleneck, grad_rows.reshape(images, slot_count, grad_rows.shape[-1])


def on_device(
    teacher_feat,
    teacher_bottleneck,
    teacher_proto,
    student_feat,
    student_bottleneck,
    student_proto,
    mask_index,
    mask_count,
    *,
    parts,
    group,
):
    images, masked = mask_index.shape
    full = images * (masked + 1)
    capacities = [c for c in (104, 112) if c < full] + [full]
    needed = jnp.max(jnp.sum(mask_count.reshape(parts, images) + 1, axis=-1))
    branch = sum((needed > c).astype(jnp.int32) for c in capacities[:-1])
    outs = lax.switch(
        branch,
        [functools.partial(packed_step, parts=parts, group=group, capacity=c) for c in capacities],
        teacher_feat,
        teacher_bottleneck,
        teacher_proto,
        student_feat[0],
        student_bottleneck[0],
        student_proto[0],
        mask_index,
        mask_count,
    )
    return tuple(out[None] for out in outs)


def solution(mesh):
    in_specs = (
        P(("dp", "group"), None, None),
        P(),
        P(None, "dp"),
        P("group", "dp", None, None),
        P("group", None, None),
        P("group", None, "dp"),
        P("dp", None),
        P(),
    )
    out_specs = (P("group", None, "dp"), P("group", "dp", None), P("group", "dp", None, None))
    step = functools.partial(on_device, parts=mesh.shape["dp"], group=mesh.shape["group"])
    return jax.shard_map(step, mesh=mesh, in_specs=in_specs, out_specs=out_specs, check_vma=False)
```

```python
import functools

import jax
import jax.numpy as jnp
from jax import lax
from jax.experimental import pallas as pl
from jax.experimental.pallas import tpu as pltpu
from jax.sharding import PartitionSpec as P

teacher_temp = 0.05
student_temp = 0.1
norm_eps = 1e-06
log2e = 1.4426950408889634
never = 1e30
bf16 = jnp.bfloat16
f32 = jnp.float32


def normalize_rows(projected):
    lengths = jnp.sqrt(jnp.sum(projected * projected, axis=-1, keepdims=True) + norm_eps)
    return (projected / lengths, lengths)


def column_of(row):
    wide = jnp.broadcast_to(row, (128, row.shape[1]))
    return jnp.transpose(wide)[:, :1]


def row_of(column):
    wide = jnp.broadcast_to(column, (column.shape[0], 128))
    return jnp.transpose(wide)[:1, :]


def vmem(megabytes):
    return pltpu.CompilerParams(vmem_limit_bytes=megabytes * 2**20)


def row_block(block, width):
    return pl.BlockSpec((block, width), lambda i: (i, 0))


def lane_block(block):
    return pl.BlockSpec((1, 1, block), lambda i: (i, 0, 0))


def whole(array):
    return pl.BlockSpec(array.shape, lambda i: (0,) * array.ndim)


def times_transposed(left, right):
    return lax.dot_general(left, right, (((1,), (1,)), ((), ())), preferred_element_type=f32)


def powers_of(scale, rows_ref, proto_ref, peak_ref, lse_ref, powers_ref):
    logits = jnp.dot(rows_ref[...], proto_ref[...], preferred_element_type=f32)
    peak = jnp.max(logits, axis=-1, keepdims=True) * scale
    powers = jnp.exp2(logits * scale - peak)
    powers_ref[...] = powers.astype(bf16)
    total = jnp.sum(powers, axis=-1, keepdims=True)
    peak_ref[0] = row_of(peak)
    lse_ref[0] = row_of(peak + jnp.log2(total))


def powers_terms_kernel(scale, rows_ref, proto_ref, peak_ref, lse_ref, powers_ref, terms_ref):
    powers_of(scale, rows_ref, proto_ref, peak_ref, lse_ref, powers_ref)
    terms_ref[...] = times_transposed(powers_ref[...], proto_ref[...]).astype(bf16)


def stored_powers(rows, proto, temp, block, fused):
    count, width = rows.shape
    columns = proto.shape[1]
    steps = count // block
    lanes = jax.ShapeDtypeStruct((steps, 1, block), f32)
    specs = [lane_block(block), lane_block(block), row_block(block, columns), row_block(block, width)]
    shapes = [lanes, lanes, jax.ShapeDtypeStruct((count, columns), bf16), jax.ShapeDtypeStruct((count, width), bf16)]
    peak, lse, *stored = pl.pallas_call(
        functools.partial(powers_terms_kernel if fused else powers_of, log2e / temp),
        grid=(steps,),
        in_specs=[row_block(block, width), whole(proto)],
        out_specs=specs if fused else specs[:3],
        out_shape=shapes if fused else shapes[:3],
        compiler_params=vmem(56 if fused else 48),
        cost_estimate=pl.CostEstimate(
            flops=2 * (1 + fused) * count * proto.size, bytes_accessed=2 * count * columns, transcendentals=count * columns
        ),
    )(rows, proto)
    return peak, lse, *stored


def terms_kernel(powers_ref, proto_ref, terms_ref):
    terms_ref[...] = times_transposed(powers_ref[...], proto_ref[...]).astype(bf16)


def row_terms(powers, proto, block):
    count, columns = powers.shape
    width = proto.shape[0]
    return pl.pallas_call(
        terms_kernel,
        grid=(count // block,),
        in_specs=[row_block(block, columns), whole(proto)],
        out_specs=row_block(block, width),
        out_shape=jax.ShapeDtypeStruct((count, width), bf16),
        compiler_params=vmem(56),
        cost_estimate=pl.CostEstimate(flops=2 * count * proto.size, bytes_accessed=2 * count * columns, transcendentals=0),
    )(powers, proto)


def total_lse(parts_lse):
    top = jnp.max(parts_lse, axis=0)
    return top + jnp.log2(jnp.sum(jnp.exp2(parts_lse - top), axis=0))


def combine_kernel(lse_s_ref, lse_t_ref, peak_s_ref, peak_t_ref, weight_ref, terms_s_ref, terms_t_ref,
                   out_ref, scale_s_ref, scale_t_ref):
    scale_s = jnp.exp2(peak_s_ref[0] - total_lse(lse_s_ref[:, 0]) + weight_ref[0])
    scale_t = jnp.exp2(peak_t_ref[0] - total_lse(lse_t_ref[:, 0]) + weight_ref[0])
    scale_s_ref[0] = scale_s
    scale_t_ref[0] = scale_t
    student = column_of(scale_s) * terms_s_ref[...].astype(f32)
    teacher = column_of(scale_t) * terms_t_ref[...].astype(f32)
    out_ref[...] = (student - teacher).astype(bf16)


def combined_terms(every_lse, peak_s, peak_t, log_weight, terms_s, terms_t):
    count, width = terms_s.shape
    steps, _, block = peak_s.shape
    parts = every_lse.shape[0]
    lanes = jax.ShapeDtypeStruct(peak_s.shape, f32)
    return pl.pallas_call(
        combine_kernel,
        grid=(steps,),
        in_specs=[
            pl.BlockSpec((parts, 1, 1, block), lambda i: (0, i, 0, 0)),
            pl.BlockSpec((parts, 1, 1, block), lambda i: (0, i + steps, 0, 0)),
            lane_block(block),
            lane_block(block),
            lane_block(block),
            row_block(block, width),
            row_block(block, width),
        ],
        out_specs=[row_block(block, width), lane_block(block), lane_block(block)],
        out_shape=[jax.ShapeDtypeStruct((count, width), bf16), lanes, lanes],
        compiler_params=vmem(52),
        cost_estimate=pl.CostEstimate(flops=3 * count * width, bytes_accessed=6 * count * width, transcendentals=64 * count),
    )(every_lse, every_lse, peak_s, peak_t, log_weight, terms_s, terms_t)


def grads_kernel(tile, student_ref, scale_s_ref, scale_t_ref, powers_s_ref, powers_t_ref, grad_ref):
    @pl.when(pl.program_id(0) == 0)
    def _():
        grad_ref[...] = jnp.zeros_like(grad_ref)

    student_T = jnp.transpose(student_ref[...])
    scale_s, scale_t = column_of(scale_s_ref[0]), column_of(scale_t_ref[0])
    for start in range(0, grad_ref.shape[1], tile):
        cols = slice(start, start + tile)
        grad = scale_s * powers_s_ref[:, cols].astype(f32) - scale_t * powers_t_ref[:, cols].astype(f32)
        grad_ref[:, cols] += jnp.dot(student_T, grad.astype(bf16), preferred_element_type=f32)


def proto_gradient(student, scale_s, scale_t, powers_s, powers_t, block, tile=512):
    count, width = student.shape
    columns = powers_s.shape[1]
    steps = count // block
    return pl.pallas_call(
        functools.partial(grads_kernel, tile),
        grid=(steps,),
        in_specs=[row_block(block, width), lane_block(block), lane_block(block), row_block(block, columns), row_block(block, columns)],
        out_specs=pl.BlockSpec((width, columns), lambda i: (0, 0)),
        out_shape=jax.ShapeDtypeStruct((width, columns), f32),
        compiler_params=vmem(56),
        cost_estimate=pl.CostEstimate(
            flops=2 * count * width * columns, bytes_accessed=4 * count * columns, transcendentals=0
        ),
    )(student, scale_s, scale_t, powers_s, powers_t)


def to_all(block, parts):
    return lax.all_to_all(jnp.broadcast_to(block[None], (parts,) + block.shape), "dp", 0, 0)


def slots_of(counts, capacity):
    lengths = counts + 1
    ends = jnp.cumsum(lengths, axis=-1)
    starts = ends - lengths
    slot = jnp.arange(capacity)[None, :, None]
    inside = (slot >= starts[:, None, :]) & (slot < ends[:, None, :])
    live = jnp.any(inside, axis=-1)
    image = jnp.sum(jnp.where(inside, jnp.arange(counts.shape[1]), 0), axis=-1)
    place = jnp.sum(jnp.where(inside, slot - starts[:, None, :], 0), axis=-1)
    share = jnp.sum(jnp.where(inside, 1.0 / counts.astype(f32)[:, None, :], 0.0), axis=-1)
    return image, place, jnp.where(place == 0, 1.0, share), live


def packed_step(
    teacher_feat,
    teacher_bottleneck,
    teacher_proto,
    student_feat,
    student_bottleneck,
    student_proto,
    mask_index,
    mask_count,
    *,
    parts,
    group,
    capacity,
):
    images, masked = mask_index.shape
    slot_count = masked + 1
    width = student_bottleneck.shape[-1]
    teacher_images = teacher_feat.shape[0]
    teacher_count = teacher_images * slot_count
    padded_count = -(-teacher_count // 16) * 16
    block = 8 * capacity if capacity < 110 else 4 * capacity if capacity < 120 else 256
    me = lax.axis_index("dp")
    indices = jnp.concatenate([jnp.zeros((images, 1), jnp.int32), mask_index], axis=1)

    image, place, weight, live = slots_of(mask_count.reshape(parts, images), capacity)
    log_weight = jnp.where(live, jnp.log2(weight / student_temp), -never).reshape(-1)
    mine = lambda array: lax.dynamic_index_in_dim(array, me, 0, keepdims=False)
    my_image, my_place, my_live = mine(image), mine(place), mine(live)
    spread = ((my_image * slot_count + my_place)[:, None] == jnp.arange(images * slot_count)) & my_live[:, None]
    my_rows = jnp.sum(jnp.where(spread, indices.reshape(1, -1), 0), axis=-1)
    spread = spread.astype(bf16)

    student_rows = student_feat[my_image, my_rows]
    student_float, lengths = normalize_rows(jnp.dot(student_rows, student_bottleneck, preferred_element_type=f32))
    student_unit = student_float.astype(bf16)
    every_student = to_all(student_unit, parts).reshape(-1, width)

    first_image = lax.axis_index("group") * teacher_images
    teacher_index = lax.dynamic_slice_in_dim(indices, first_image, teacher_images, 0)
    teacher_rows = teacher_feat[jnp.arange(teacher_images)[:, None], teacher_index].reshape(-1, teacher_feat.shape[-1])
    teacher_unit = normalize_rows(jnp.dot(teacher_rows, teacher_bottleneck, preferred_element_type=f32))[0].astype(bf16)
    teacher_unit = jnp.pad(teacher_unit, ((0, padded_count - teacher_count), (0, 0)))
    others = [lax.ppermute(teacher_unit, "group", [(i, i ^ k) for i in range(group)]) for k in range(1, group)]
    group_teacher = jnp.concatenate([teacher_unit] + others)
    owner = (my_image // teacher_images) ^ lax.axis_index("group")
    held = owner * padded_count + (my_image % teacher_images) * slot_count + my_place
    picks = ((held[:, None] == jnp.arange(group * padded_count)) & my_live[:, None]).astype(bf16)
    group_teacher = jnp.dot(picks, group_teacher, preferred_element_type=f32).astype(bf16)
    group_teacher, every_student = lax.optimization_barrier((group_teacher, every_student))
    every_teacher = to_all(group_teacher, parts).reshape(-1, width)

    peak_s, lse_s, powers_s, terms_s = stored_powers(every_student, student_proto, student_temp, block, True)
    every_teacher, terms_s = lax.optimization_barrier((every_teacher, terms_s))
    peak_t, lse_t, powers_t = stored_powers(every_teacher, teacher_proto, teacher_temp, block, False)
    every_lse = to_all(jnp.concatenate([lse_s, lse_t]), parts)
    terms_t = row_terms(powers_t, student_proto, block)
    every_lse, terms_t = lax.optimization_barrier((every_lse, terms_t))
    my_terms, scale_s, scale_t = combined_terms(
        every_lse, peak_s, peak_t, log_weight.reshape(peak_s.shape), terms_s, terms_t
    )
    terms = lax.all_to_all(my_terms.reshape(parts, capacity, width), "dp", 0, 0)
    grad_proto = proto_gradient(every_student, scale_s, scale_t, powers_s, powers_t, block)
    terms, grad_proto = lax.optimization_barrier((terms, grad_proto))
    feature_grad = jnp.sum(terms.astype(f32), axis=0)
    along_unit = jnp.sum(student_float * feature_grad, axis=-1, keepdims=True)
    unit_grad = ((feature_grad - student_float * along_unit) / lengths).astype(bf16)
    partial_bottleneck = lax.dot_general(
        student_rows, unit_grad, (((0,), (0,)), ((), ())), preferred_element_type=f32
    ).astype(bf16)
    pieces = lax.all_to_all(partial_bottleneck.reshape(parts, -1, width), "dp", 0, 0)
    grad_bottleneck = jnp.sum(pieces.astype(f32), axis=0)
    spread_grad = lax.dot_general(
        spread, unit_grad, (((0,), (0,)), ((), ())), preferred_element_type=f32
    ).astype(bf16)
    grad_rows = lax.dot_general(
        spread_grad, student_bottleneck, (((1,), (1,)), ((), ())), preferred_element_type=f32
    ).astype(bf16)
    return grad_proto, grad_bottleneck, grad_rows.reshape(images, slot_count, grad_rows.shape[-1])


def on_device(
    teacher_feat,
    teacher_bottleneck,
    teacher_proto,
    student_feat,
    student_bottleneck,
    student_proto,
    mask_index,
    mask_count,
    *,
    parts,
    group,
):
    images, masked = mask_index.shape
    full = images * (masked + 1)
    capacities = [c for c in (104, 112) if c < full] + [full]
    needed = jnp.max(jnp.sum(mask_count.reshape(parts, images) + 1, axis=-1))
    branch = sum((needed > c).astype(jnp.int32) for c in capacities[:-1])
    outs = lax.switch(
        branch,
        [functools.partial(packed_step, parts=parts, group=group, capacity=c) for c in capacities],
        teacher_feat,
        teacher_bottleneck,
        teacher_proto,
        student_feat[0],
        student_bottleneck[0],
        student_proto[0],
        mask_index,
        mask_count,
    )
    return tuple(out[None] for out in outs)


def solution(mesh):
    in_specs = (
        P(("dp", "group"), None, None),
        P(),
        P(None, "dp"),
        P("group", "dp", None, None),
        P("group", None, None),
        P("group", None, "dp"),
        P("dp", None),
        P(),
    )
    out_specs = (P("group", None, "dp"), P("group", "dp", None), P("group", "dp", None, None))
    step = functools.partial(on_device, parts=mesh.shape["dp"], group=mesh.shape["group"])
    return jax.shard_map(step, mesh=mesh, in_specs=in_specs, out_specs=out_specs, check_vma=False)
```

```python
import functools

import jax
import jax.numpy as jnp
from jax import lax
from jax.experimental import pallas as pl
from jax.experimental.pallas import tpu as pltpu
from jax.sharding import PartitionSpec as P

teacher_temp = 0.05
student_temp = 0.1
norm_eps = 1e-06
log2e = 1.4426950408889634
never = 1e30
bf16 = jnp.bfloat16
f32 = jnp.float32


def normalize_rows(projected):
    lengths = jnp.sqrt(jnp.sum(projected * projected, axis=-1, keepdims=True) + norm_eps)
    return (projected / lengths, lengths)


def column_of(row):
    wide = jnp.broadcast_to(row, (128, row.shape[1]))
    return jnp.transpose(wide)[:, :1]


def row_of(column):
    wide = jnp.broadcast_to(column, (column.shape[0], 128))
    return jnp.transpose(wide)[:1, :]


def vmem(megabytes):
    return pltpu.CompilerParams(vmem_limit_bytes=megabytes * 2**20)


def row_block(block, width):
    return pl.BlockSpec((block, width), lambda i: (i, 0))


def lane_block(block):
    return pl.BlockSpec((1, 1, block), lambda i: (i, 0, 0))


def whole(array):
    return pl.BlockSpec(array.shape, lambda i: (0,) * array.ndim)


def times_transposed(left, right):
    return lax.dot_general(left, right, (((1,), (1,)), ((), ())), preferred_element_type=f32)


def powers_of(scale, rows_ref, proto_ref, peak_ref, lse_ref, powers_ref):
    logits = jnp.dot(rows_ref[...], proto_ref[...], preferred_element_type=f32)
    peak = jnp.max(logits, axis=-1, keepdims=True) * scale
    powers = jnp.exp2(logits * scale - peak)
    powers_ref[...] = powers.astype(bf16)
    total = jnp.sum(powers, axis=-1, keepdims=True)
    peak_ref[0] = row_of(peak)
    lse_ref[0] = row_of(peak + jnp.log2(total))


def powers_terms_kernel(scale, rows_ref, proto_ref, peak_ref, lse_ref, powers_ref, terms_ref):
    powers_of(scale, rows_ref, proto_ref, peak_ref, lse_ref, powers_ref)
    terms_ref[...] = times_transposed(powers_ref[...], proto_ref[...]).astype(bf16)


def stored_powers(rows, proto, temp, block, fused):
    count, width = rows.shape
    columns = proto.shape[1]
    steps = count // block
    lanes = jax.ShapeDtypeStruct((steps, 1, block), f32)
    specs = [lane_block(block), lane_block(block), row_block(block, columns), row_block(block, width)]
    shapes = [lanes, lanes, jax.ShapeDtypeStruct((count, columns), bf16), jax.ShapeDtypeStruct((count, width), bf16)]
    peak, lse, *stored = pl.pallas_call(
        functools.partial(powers_terms_kernel if fused else powers_of, log2e / temp),
        grid=(steps,),
        in_specs=[row_block(block, width), whole(proto)],
        out_specs=specs if fused else specs[:3],
        out_shape=shapes if fused else shapes[:3],
        compiler_params=vmem(56 if fused else 48),
        cost_estimate=pl.CostEstimate(
            flops=2 * (1 + fused) * count * proto.size, bytes_accessed=2 * count * columns, transcendentals=count * columns
        ),
    )(rows, proto)
    return peak, lse, *stored


def terms_kernel(powers_ref, proto_ref, terms_ref):
    terms_ref[...] = times_transposed(powers_ref[...], proto_ref[...]).astype(bf16)


def row_terms(powers, proto, block):
    count, columns = powers.shape
    width = proto.shape[0]
    return pl.pallas_call(
        terms_kernel,
        grid=(count // block,),
        in_specs=[row_block(block, columns), whole(proto)],
        out_specs=row_block(block, width),
        out_shape=jax.ShapeDtypeStruct((count, width), bf16),
        compiler_params=vmem(56),
        cost_estimate=pl.CostEstimate(flops=2 * count * proto.size, bytes_accessed=2 * count * columns, transcendentals=0),
    )(powers, proto)


def total_lse(parts_lse):
    top = jnp.max(parts_lse, axis=0)
    return top + jnp.log2(jnp.sum(jnp.exp2(parts_lse - top), axis=0))


def combine_kernel(lse_s_ref, lse_t_ref, peak_s_ref, peak_t_ref, weight_ref, terms_s_ref, terms_t_ref,
                   out_ref, scale_s_ref, scale_t_ref):
    scale_s = jnp.exp2(peak_s_ref[0] - total_lse(lse_s_ref[:, 0]) + weight_ref[0])
    scale_t = jnp.exp2(peak_t_ref[0] - total_lse(lse_t_ref[:, 0]) + weight_ref[0])
    scale_s_ref[0] = scale_s
    scale_t_ref[0] = scale_t
    student = column_of(scale_s) * terms_s_ref[...].astype(f32)
    teacher = column_of(scale_t) * terms_t_ref[...].astype(f32)
    out_ref[...] = (student - teacher).astype(bf16)


def combined_terms(every_lse, peak_s, peak_t, log_weight, terms_s, terms_t):
    count, width = terms_s.shape
    steps, _, block = peak_s.shape
    parts = every_lse.shape[0]
    lanes = jax.ShapeDtypeStruct(peak_s.shape, f32)
    return pl.pallas_call(
        combine_kernel,
        grid=(steps,),
        in_specs=[
            pl.BlockSpec((parts, 1, 1, block), lambda i: (0, i, 0, 0)),
            pl.BlockSpec((parts, 1, 1, block), lambda i: (0, i + steps, 0, 0)),
            lane_block(block),
            lane_block(block),
            lane_block(block),
            row_block(block, width),
            row_block(block, width),
        ],
        out_specs=[row_block(block, width), lane_block(block), lane_block(block)],
        out_shape=[jax.ShapeDtypeStruct((count, width), bf16), lanes, lanes],
        compiler_params=vmem(52),
        cost_estimate=pl.CostEstimate(flops=3 * count * width, bytes_accessed=6 * count * width, transcendentals=64 * count),
    )(every_lse, every_lse, peak_s, peak_t, log_weight, terms_s, terms_t)


def grads_kernel(tile, student_ref, scale_s_ref, scale_t_ref, powers_s_ref, powers_t_ref, grad_ref):
    @pl.when(pl.program_id(0) == 0)
    def _():
        grad_ref[...] = jnp.zeros_like(grad_ref)

    student_T = jnp.transpose(student_ref[...])
    scale_s, scale_t = column_of(scale_s_ref[0]), column_of(scale_t_ref[0])
    for start in range(0, grad_ref.shape[1], tile):
        cols = slice(start, start + tile)
        grad = scale_s * powers_s_ref[:, cols].astype(f32) - scale_t * powers_t_ref[:, cols].astype(f32)
        grad_ref[:, cols] += jnp.dot(student_T, grad.astype(bf16), preferred_element_type=f32)


def proto_gradient(student, scale_s, scale_t, powers_s, powers_t, block, tile=512):
    count, width = student.shape
    columns = powers_s.shape[1]
    steps = count // block
    return pl.pallas_call(
        functools.partial(grads_kernel, tile),
        grid=(steps,),
        in_specs=[row_block(block, width), lane_block(block), lane_block(block), row_block(block, columns), row_block(block, columns)],
        out_specs=pl.BlockSpec((width, columns), lambda i: (0, 0)),
        out_shape=jax.ShapeDtypeStruct((width, columns), f32),
        compiler_params=vmem(56),
        cost_estimate=pl.CostEstimate(
            flops=2 * count * width * columns, bytes_accessed=4 * count * columns, transcendentals=0
        ),
    )(student, scale_s, scale_t, powers_s, powers_t)


def to_all(block, parts):
    return lax.all_to_all(jnp.broadcast_to(block[None], (parts,) + block.shape), "dp", 0, 0)


def slots_of(counts, capacity):
    lengths = counts + 1
    ends = jnp.cumsum(lengths, axis=-1)
    starts = ends - lengths
    slot = jnp.arange(capacity)[None, :, None]
    inside = (slot >= starts[:, None, :]) & (slot < ends[:, None, :])
    live = jnp.any(inside, axis=-1)
    image = jnp.sum(jnp.where(inside, jnp.arange(counts.shape[1]), 0), axis=-1)
    place = jnp.sum(jnp.where(inside, slot - starts[:, None, :], 0), axis=-1)
    share = jnp.sum(jnp.where(inside, 1.0 / counts.astype(f32)[:, None, :], 0.0), axis=-1)
    return image, place, jnp.where(place == 0, 1.0, share), live


def packed_step(
    teacher_feat,
    teacher_bottleneck,
    teacher_proto,
    student_feat,
    student_bottleneck,
    student_proto,
    mask_index,
    mask_count,
    *,
    parts,
    group,
    capacity,
):
    images, masked = mask_index.shape
    slot_count = masked + 1
    width = student_bottleneck.shape[-1]
    teacher_images = teacher_feat.shape[0]
    teacher_count = teacher_images * slot_count
    padded_count = -(-teacher_count // 16) * 16
    block = 8 * capacity if capacity < 110 else 4 * capacity if capacity < 120 else 256
    me = lax.axis_index("dp")
    indices = jnp.concatenate([jnp.zeros((images, 1), jnp.int32), mask_index], axis=1)

    image, place, weight, live = slots_of(mask_count.reshape(parts, images), capacity)
    log_weight = jnp.where(live, jnp.log2(weight / student_temp), -never).reshape(-1)
    mine = lambda array: lax.dynamic_index_in_dim(array, me, 0, keepdims=False)
    my_image, my_place, my_live = mine(image), mine(place), mine(live)
    spread = ((my_image * slot_count + my_place)[:, None] == jnp.arange(images * slot_count)) & my_live[:, None]
    my_rows = jnp.sum(jnp.where(spread, indices.reshape(1, -1), 0), axis=-1)
    spread = spread.astype(bf16)

    student_rows = student_feat[my_image, my_rows]
    student_float, lengths = normalize_rows(jnp.dot(student_rows, student_bottleneck, preferred_element_type=f32))
    student_unit = student_float.astype(bf16)

    first_image = lax.axis_index("group") * teacher_images
    teacher_index = lax.dynamic_slice_in_dim(indices, first_image, teacher_images, 0)
    teacher_rows = teacher_feat[jnp.arange(teacher_images)[:, None], teacher_index].reshape(-1, teacher_feat.shape[-1])
    teacher_unit = normalize_rows(jnp.dot(teacher_rows, teacher_bottleneck, preferred_element_type=f32))[0].astype(bf16)
    teacher_unit = jnp.pad(teacher_unit, ((0, padded_count - teacher_count), (0, 0)))
    others = [lax.ppermute(teacher_unit, "group", [(i, i ^ k) for i in range(group)]) for k in range(1, group)]
    group_teacher = jnp.concatenate([teacher_unit] + others)
    owner = (my_image // teacher_images) ^ lax.axis_index("group")
    held = owner * padded_count + (my_image % teacher_images) * slot_count + my_place
    picks = ((held[:, None] == jnp.arange(group * padded_count)) & my_live[:, None]).astype(bf16)
    group_teacher = jnp.dot(picks, group_teacher, preferred_element_type=f32).astype(bf16)
    group_teacher, student_unit = lax.optimization_barrier((group_teacher, student_unit))
    every_student = to_all(student_unit, parts).reshape(-1, width)
    copies = jnp.broadcast_to(group_teacher[None], (parts,) + group_teacher.shape)
    copies, every_student = lax.optimization_barrier((copies, every_student))
    every_teacher = lax.all_to_all(copies, "dp", 0, 0).reshape(-1, width)

    peak_s, lse_s, powers_s, terms_s = stored_powers(every_student, student_proto, student_temp, block, True)
    every_teacher, terms_s = lax.optimization_barrier((every_teacher, terms_s))
    peak_t, lse_t, powers_t = stored_powers(every_teacher, teacher_proto, teacher_temp, block, False)
    every_lse = to_all(jnp.concatenate([lse_s, lse_t]), parts)
    terms_t = row_terms(powers_t, student_proto, block)
    every_lse, terms_t = lax.optimization_barrier((every_lse, terms_t))
    my_terms, scale_s, scale_t = combined_terms(
        every_lse, peak_s, peak_t, log_weight.reshape(peak_s.shape), terms_s, terms_t
    )
    terms = lax.all_to_all(my_terms.reshape(parts, capacity, width), "dp", 0, 0)
    grad_proto = proto_gradient(every_student, scale_s, scale_t, powers_s, powers_t, block)
    terms, grad_proto = lax.optimization_barrier((terms, grad_proto))
    feature_grad = jnp.sum(terms.astype(f32), axis=0)
    along_unit = jnp.sum(student_float * feature_grad, axis=-1, keepdims=True)
    unit_grad = ((feature_grad - student_float * along_unit) / lengths).astype(bf16)
    partial_bottleneck = lax.dot_general(
        student_rows, unit_grad, (((0,), (0,)), ((), ())), preferred_element_type=f32
    ).astype(bf16)
    pieces = lax.all_to_all(partial_bottleneck.reshape(parts, -1, width), "dp", 0, 0)
    grad_bottleneck = jnp.sum(pieces.astype(f32), axis=0)
    spread_grad = lax.dot_general(
        spread, unit_grad, (((0,), (0,)), ((), ())), preferred_element_type=f32
    ).astype(bf16)
    grad_rows = lax.dot_general(
        spread_grad, student_bottleneck, (((1,), (1,)), ((), ())), preferred_element_type=f32
    ).astype(bf16)
    return grad_proto, grad_bottleneck, grad_rows.reshape(images, slot_count, grad_rows.shape[-1])


def on_device(
    teacher_feat,
    teacher_bottleneck,
    teacher_proto,
    student_feat,
    student_bottleneck,
    student_proto,
    mask_index,
    mask_count,
    *,
    parts,
    group,
):
    images, masked = mask_index.shape
    full = images * (masked + 1)
    capacities = [c for c in (104, 112) if c < full] + [full]
    needed = jnp.max(jnp.sum(mask_count.reshape(parts, images) + 1, axis=-1))
    branch = sum((needed > c).astype(jnp.int32) for c in capacities[:-1])
    outs = lax.switch(
        branch,
        [functools.partial(packed_step, parts=parts, group=group, capacity=c) for c in capacities],
        teacher_feat,
        teacher_bottleneck,
        teacher_proto,
        student_feat[0],
        student_bottleneck[0],
        student_proto[0],
        mask_index,
        mask_count,
    )
    return tuple(out[None] for out in outs)


def solution(mesh):
    in_specs = (
        P(("dp", "group"), None, None),
        P(),
        P(None, "dp"),
        P("group", "dp", None, None),
        P("group", None, None),
        P("group", None, "dp"),
        P("dp", None),
        P(),
    )
    out_specs = (P("group", None, "dp"), P("group", "dp", None), P("group", "dp", None, None))
    step = functools.partial(on_device, parts=mesh.shape["dp"], group=mesh.shape["group"])
    return jax.shard_map(step, mesh=mesh, in_specs=in_specs, out_specs=out_specs, check_vma=False)
```

```python
import functools

import jax
import jax.numpy as jnp
from jax import lax
from jax.experimental import pallas as pl
from jax.experimental.pallas import tpu as pltpu
from jax.sharding import PartitionSpec as P

teacher_temp = 0.05
student_temp = 0.1
norm_eps = 1e-06
log2e = 1.4426950408889634
never = 1e30
bf16 = jnp.bfloat16
f32 = jnp.float32


def normalize_rows(projected):
    lengths = jnp.sqrt(jnp.sum(projected * projected, axis=-1, keepdims=True) + norm_eps)
    return (projected / lengths, lengths)


def column_of(row):
    wide = jnp.broadcast_to(row, (128, row.shape[1]))
    return jnp.transpose(wide)[:, :1]


def row_of(column):
    wide = jnp.broadcast_to(column, (column.shape[0], 128))
    return jnp.transpose(wide)[:1, :]


def vmem(megabytes):
    return pltpu.CompilerParams(vmem_limit_bytes=megabytes * 2**20)


def row_block(block, width):
    return pl.BlockSpec((block, width), lambda i: (i, 0))


def lane_block(block):
    return pl.BlockSpec((1, 1, block), lambda i: (i, 0, 0))


def whole(array):
    return pl.BlockSpec(array.shape, lambda i: (0,) * array.ndim)


def times_transposed(left, right):
    return lax.dot_general(left, right, (((1,), (1,)), ((), ())), preferred_element_type=f32)


def powers_of(scale, rows_ref, proto_ref, peak_ref, lse_ref, powers_ref):
    logits = jnp.dot(rows_ref[...], proto_ref[...], preferred_element_type=f32)
    peak = jnp.max(logits, axis=-1, keepdims=True) * scale
    powers = jnp.exp2(logits * scale - peak)
    powers_ref[...] = powers.astype(bf16)
    total = jnp.sum(powers, axis=-1, keepdims=True)
    peak_ref[0] = row_of(peak)
    lse_ref[0] = row_of(peak + jnp.log2(total))


def powers_terms_kernel(scale, rows_ref, proto_ref, peak_ref, lse_ref, powers_ref, terms_ref):
    powers_of(scale, rows_ref, proto_ref, peak_ref, lse_ref, powers_ref)
    terms_ref[...] = times_transposed(powers_ref[...], proto_ref[...]).astype(bf16)


def stored_powers(rows, proto, temp, block, fused):
    count, width = rows.shape
    columns = proto.shape[1]
    steps = count // block
    lanes = jax.ShapeDtypeStruct((steps, 1, block), f32)
    specs = [lane_block(block), lane_block(block), row_block(block, columns), row_block(block, width)]
    shapes = [lanes, lanes, jax.ShapeDtypeStruct((count, columns), bf16), jax.ShapeDtypeStruct((count, width), bf16)]
    peak, lse, *stored = pl.pallas_call(
        functools.partial(powers_terms_kernel if fused else powers_of, log2e / temp),
        grid=(steps,),
        in_specs=[row_block(block, width), whole(proto)],
        out_specs=specs if fused else specs[:3],
        out_shape=shapes if fused else shapes[:3],
        compiler_params=vmem(56 if fused else 48),
        cost_estimate=pl.CostEstimate(
            flops=2 * (1 + fused) * count * proto.size, bytes_accessed=2 * count * columns, transcendentals=count * columns
        ),
    )(rows, proto)
    return peak, lse, *stored


def terms_kernel(powers_ref, proto_ref, terms_ref):
    terms_ref[...] = times_transposed(powers_ref[...], proto_ref[...]).astype(bf16)


def row_terms(powers, proto, block):
    count, columns = powers.shape
    width = proto.shape[0]
    return pl.pallas_call(
        terms_kernel,
        grid=(count // block,),
        in_specs=[row_block(block, columns), whole(proto)],
        out_specs=row_block(block, width),
        out_shape=jax.ShapeDtypeStruct((count, width), bf16),
        compiler_params=vmem(56),
        cost_estimate=pl.CostEstimate(flops=2 * count * proto.size, bytes_accessed=2 * count * columns, transcendentals=0),
    )(powers, proto)


def total_lse(parts_lse):
    top = jnp.max(parts_lse, axis=0, keepdims=True)
    return top + jnp.log2(jnp.sum(jnp.exp2(parts_lse - top), axis=0, keepdims=True))


def combine_kernel(lse_s_ref, lse_t_ref, peak_s_ref, peak_t_ref, weight_ref, terms_s_ref, terms_t_ref,
                   out_ref, scale_s_ref, scale_t_ref):
    scale_s = jnp.exp2(peak_s_ref[0] - total_lse(lse_s_ref[:, 0, 0]) + weight_ref[0])
    scale_t = jnp.exp2(peak_t_ref[0] - total_lse(lse_t_ref[:, 0, 0]) + weight_ref[0])
    scale_s_ref[0] = scale_s
    scale_t_ref[0] = scale_t
    student = column_of(scale_s) * terms_s_ref[...].astype(f32)
    teacher = column_of(scale_t) * terms_t_ref[...].astype(f32)
    out_ref[...] = (student - teacher).astype(bf16)


def combined_terms(every_lse, peak_s, peak_t, log_weight, terms_s, terms_t):
    count, width = terms_s.shape
    steps, _, block = peak_s.shape
    parts = every_lse.shape[0]
    lanes = jax.ShapeDtypeStruct(peak_s.shape, f32)
    return pl.pallas_call(
        combine_kernel,
        grid=(steps,),
        in_specs=[
            pl.BlockSpec((parts, 1, 1, block), lambda i: (0, i, 0, 0)),
            pl.BlockSpec((parts, 1, 1, block), lambda i: (0, i + steps, 0, 0)),
            lane_block(block),
            lane_block(block),
            lane_block(block),
            row_block(block, width),
            row_block(block, width),
        ],
        out_specs=[row_block(block, width), lane_block(block), lane_block(block)],
        out_shape=[jax.ShapeDtypeStruct((count, width), bf16), lanes, lanes],
        compiler_params=vmem(52),
        cost_estimate=pl.CostEstimate(flops=3 * count * width, bytes_accessed=6 * count * width, transcendentals=64 * count),
    )(every_lse, every_lse, peak_s, peak_t, log_weight, terms_s, terms_t)


def grads_kernel(tile, student_ref, scale_s_ref, scale_t_ref, powers_s_ref, powers_t_ref, grad_ref):
    @pl.when(pl.program_id(0) == 0)
    def _():
        grad_ref[...] = jnp.zeros_like(grad_ref)

    student_T = jnp.transpose(student_ref[...])
    scale_s, scale_t = column_of(scale_s_ref[0]), column_of(scale_t_ref[0])
    for start in range(0, grad_ref.shape[1], tile):
        cols = slice(start, start + tile)
        grad = scale_s * powers_s_ref[:, cols].astype(f32) - scale_t * powers_t_ref[:, cols].astype(f32)
        grad_ref[:, cols] += jnp.dot(student_T, grad.astype(bf16), preferred_element_type=f32)


def proto_gradient(student, scale_s, scale_t, powers_s, powers_t, block, tile=512):
    count, width = student.shape
    columns = powers_s.shape[1]
    steps = count // block
    return pl.pallas_call(
        functools.partial(grads_kernel, tile),
        grid=(steps,),
        in_specs=[row_block(block, width), lane_block(block), lane_block(block), row_block(block, columns), row_block(block, columns)],
        out_specs=pl.BlockSpec((width, columns), lambda i: (0, 0)),
        out_shape=jax.ShapeDtypeStruct((width, columns), f32),
        compiler_params=vmem(56),
        cost_estimate=pl.CostEstimate(
            flops=2 * count * width * columns, bytes_accessed=4 * count * columns, transcendentals=0
        ),
    )(student, scale_s, scale_t, powers_s, powers_t)


def to_all(block, parts):
    return lax.all_to_all(jnp.broadcast_to(block[None], (parts,) + block.shape), "dp", 0, 0)


def slots_of(counts, capacity):
    lengths = counts + 1
    ends = jnp.cumsum(lengths, axis=-1)
    starts = ends - lengths
    slot = jnp.arange(capacity)[None, :, None]
    inside = (slot >= starts[:, None, :]) & (slot < ends[:, None, :])
    live = jnp.any(inside, axis=-1)
    image = jnp.sum(jnp.where(inside, jnp.arange(counts.shape[1]), 0), axis=-1)
    place = jnp.sum(jnp.where(inside, slot - starts[:, None, :], 0), axis=-1)
    share = jnp.sum(jnp.where(inside, 1.0 / counts.astype(f32)[:, None, :], 0.0), axis=-1)
    return image, place, jnp.where(place == 0, 1.0, share), live


def packed_step(
    teacher_feat,
    teacher_bottleneck,
    teacher_proto,
    student_feat,
    student_bottleneck,
    student_proto,
    mask_index,
    mask_count,
    *,
    parts,
    group,
    capacity,
):
    images, masked = mask_index.shape
    slot_count = masked + 1
    width = student_bottleneck.shape[-1]
    teacher_images = teacher_feat.shape[0]
    teacher_count = teacher_images * slot_count
    padded_count = -(-teacher_count // 16) * 16
    block = 8 * capacity if capacity < 110 else 4 * capacity if capacity < 120 else 256
    me = lax.axis_index("dp")
    indices = jnp.concatenate([jnp.zeros((images, 1), jnp.int32), mask_index], axis=1)

    image, place, weight, live = slots_of(mask_count.reshape(parts, images), capacity)
    log_weight = jnp.where(live, jnp.log2(weight / student_temp), -never).reshape(-1)
    mine = lambda array: lax.dynamic_index_in_dim(array, me, 0, keepdims=False)
    my_image, my_place, my_live = mine(image), mine(place), mine(live)
    spread = ((my_image * slot_count + my_place)[:, None] == jnp.arange(images * slot_count)) & my_live[:, None]
    my_rows = jnp.sum(jnp.where(spread, indices.reshape(1, -1), 0), axis=-1)
    spread = spread.astype(bf16)

    student_rows = student_feat[my_image, my_rows]
    student_float, lengths = normalize_rows(jnp.dot(student_rows, student_bottleneck, preferred_element_type=f32))
    student_unit = student_float.astype(bf16)

    first_image = lax.axis_index("group") * teacher_images
    teacher_index = lax.dynamic_slice_in_dim(indices, first_image, teacher_images, 0)
    teacher_rows = teacher_feat[jnp.arange(teacher_images)[:, None], teacher_index].reshape(-1, teacher_feat.shape[-1])
    teacher_unit = normalize_rows(jnp.dot(teacher_rows, teacher_bottleneck, preferred_element_type=f32))[0].astype(bf16)
    teacher_unit = jnp.pad(teacher_unit, ((0, padded_count - teacher_count), (0, 0)))
    others = [lax.ppermute(teacher_unit, "group", [(i, i ^ k) for i in range(group)]) for k in range(1, group)]
    group_teacher = jnp.concatenate([teacher_unit] + others)
    owner = (my_image // teacher_images) ^ lax.axis_index("group")
    held = owner * padded_count + (my_image % teacher_images) * slot_count + my_place
    picks = ((held[:, None] == jnp.arange(group * padded_count)) & my_live[:, None]).astype(bf16)
    group_teacher = jnp.dot(picks, group_teacher, preferred_element_type=f32).astype(bf16)
    group_teacher, student_unit = lax.optimization_barrier((group_teacher, student_unit))
    every_student = to_all(student_unit, parts).reshape(-1, width)
    copies = jnp.broadcast_to(group_teacher[None], (parts,) + group_teacher.shape)
    copies, every_student = lax.optimization_barrier((copies, every_student))
    every_teacher = lax.all_to_all(copies, "dp", 0, 0).reshape(-1, width)

    peak_s, lse_s, powers_s, terms_s = stored_powers(every_student, student_proto, student_temp, block, True)
    every_teacher, terms_s = lax.optimization_barrier((every_teacher, terms_s))
    peak_t, lse_t, powers_t = stored_powers(every_teacher, teacher_proto, teacher_temp, block, False)
    every_lse = to_all(jnp.concatenate([lse_s, lse_t]), parts)
    terms_t = row_terms(powers_t, student_proto, block)
    every_lse, terms_t = lax.optimization_barrier((every_lse, terms_t))
    my_terms, scale_s, scale_t = combined_terms(
        every_lse, peak_s, peak_t, log_weight.reshape(peak_s.shape), terms_s, terms_t
    )
    terms = lax.all_to_all(my_terms.reshape(parts, capacity, width), "dp", 0, 0)
    grad_proto = proto_gradient(every_student, scale_s, scale_t, powers_s, powers_t, block)
    terms, grad_proto = lax.optimization_barrier((terms, grad_proto))
    feature_grad = jnp.sum(terms.astype(f32), axis=0)
    along_unit = jnp.sum(student_float * feature_grad, axis=-1, keepdims=True)
    unit_grad = ((feature_grad - student_float * along_unit) / lengths).astype(bf16)
    partial_bottleneck = lax.dot_general(
        student_rows, unit_grad, (((0,), (0,)), ((), ())), preferred_element_type=f32
    ).astype(bf16)
    pieces = lax.all_to_all(partial_bottleneck.reshape(parts, -1, width), "dp", 0, 0)
    grad_bottleneck = jnp.sum(pieces.astype(f32), axis=0)
    spread_grad = lax.dot_general(
        spread, unit_grad, (((0,), (0,)), ((), ())), preferred_element_type=f32
    ).astype(bf16)
    grad_rows = lax.dot_general(
        spread_grad, student_bottleneck, (((1,), (1,)), ((), ())), preferred_element_type=f32
    ).astype(bf16)
    return grad_proto, grad_bottleneck, grad_rows.reshape(images, slot_count, grad_rows.shape[-1])


def on_device(
    teacher_feat,
    teacher_bottleneck,
    teacher_proto,
    student_feat,
    student_bottleneck,
    student_proto,
    mask_index,
    mask_count,
    *,
    parts,
    group,
):
    images, masked = mask_index.shape
    full = images * (masked + 1)
    capacities = [c for c in (104, 112) if c < full] + [full]
    needed = jnp.max(jnp.sum(mask_count.reshape(parts, images) + 1, axis=-1))
    branch = sum((needed > c).astype(jnp.int32) for c in capacities[:-1])
    outs = lax.switch(
        branch,
        [functools.partial(packed_step, parts=parts, group=group, capacity=c) for c in capacities],
        teacher_feat,
        teacher_bottleneck,
        teacher_proto,
        student_feat[0],
        student_bottleneck[0],
        student_proto[0],
        mask_index,
        mask_count,
    )
    return tuple(out[None] for out in outs)


def solution(mesh):
    in_specs = (
        P(("dp", "group"), None, None),
        P(),
        P(None, "dp"),
        P("group", "dp", None, None),
        P("group", None, None),
        P("group", None, "dp"),
        P("dp", None),
        P(),
    )
    out_specs = (P("group", None, "dp"), P("group", "dp", None), P("group", "dp", None, None))
    step = functools.partial(on_device, parts=mesh.shape["dp"], group=mesh.shape["group"])
    return jax.shard_map(step, mesh=mesh, in_specs=in_specs, out_specs=out_specs, check_vma=False)
```
